512 devices in a mesh: aper: 32 (over z, core), rng: 4 (over x), ang: 4 (over y).
Axes of the slice: x: 4, y: 4, z: 16, core: 2. Of those that a mesh axis runs over, the one named last changes fastest.
Arguments:
- subimages: bfloat16 [128, 2, 1024, 512], P('aper', None, 'ang', 'rng'), may hold values from -6 to 6
- beam_offsets: int32 [3, 2, 2, 1024], P(None, None, None, 'ang'), may hold values from -4 to 0
- range_offsets: int32 [3, 2, 2, 1024], P(None, None, None, 'ang'), may hold values from -4 to 3
- beam_taps: bfloat16 [3, 2, 2, 4, 1024], P(None, None, None, None, 'ang'), may hold values from 0.14941406 to 0.59765625
- range_frac: float32 [3, 2, 2, 1024], P(None, None, None, 'ang'), may hold values from 0 to 1
- phase_base: float32 [128, 3, 2, 1024], P('aper', None, None, 'ang'), may hold values from -3.140625 to 3.140625
- phase_rate: float32 [3, 2, 1024], P(None, None, 'ang'), may hold values from -6 to 6
- final_phase: float32 [128, 1024], P(None, 'ang'), may hold values from -3.140625 to 3.140625
Outputs:
- image: float32 [2, 4, 256, 512], P(None, 'ang', 'aper', 'rng')
The draws below stay inside these ranges and needn't reach their ends.
Inputs may be any that keep to these rules, and one draw needn't show every extreme that they name: `beam_offsets`: the taps of parent beam p read child beams p + offset to p + offset + 3. `range_offsets`: range bin r reads the bins r + offset and r + offset + 1.
All inputs are finite; a program needn't handle non-finite values.
Results may differ from the reference program's by a relative error of at most 0.0046.
Values may be sent and summed in bfloat16 or wider, within the bound.
A program may use at most 64 MiB of HBM per device.

```python
import math
import jax
import jax.numpy as jnp
from jax import lax

B_DEV = 256
LEVELS = 3
TAPS = 4
HALO = 4
S = 128
NB = 1024
NR = 512
N_ANG = 4


def place_ends(values, own_key, low, largest):
    longest = values.shape.index(max(values.shape))
    spots = []
    for shift in (0, 1):
        where = [jax.random.randint(jax.random.fold_in(own_key, axis), (), 0, length) for axis, length in enumerate(values.shape)]
        where[longest] = (where[longest] + shift) % values.shape[longest]
        spots.append(tuple(where))
    return values.at[spots[0]].set(low).at[spots[1]].set(largest)


def steps_of(key, shape, shards, low, largest):
    def one(axis_at, blocks):
        draws = jax.random.uniform(jax.random.fold_in(jax.random.fold_in(key, 6), axis_at), (blocks,), jnp.float32, low / len(shards), largest / len(shards))
        return jnp.repeat(jnp.exp(draws), shape[axis_at] // blocks).reshape((-1,) + (1,) * (len(shape) - axis_at - 1))

    gain = one(*shards[0])
    for cut in shards[1:]:
        gain = gain * one(*cut)
    return gain


def normal_values(own_key, extent, width, limit, cuts=(), kind=jnp.bfloat16):
    entries = width * jax.random.normal(own_key, extent, jnp.float32)
    if cuts:
        entries = entries * steps_of(own_key, extent, cuts, -0.22, 0.18)
    return jnp.clip(entries, -limit, limit).astype(kind)


def setup_inputs(seed: int = 0) -> dict:
    keys = jax.random.split(jax.random.key(seed), 9)
    return {
        "subimages": normal_values(keys[0], (S, 2, NB, NR), 1.0, 6.0, ((0, 32), (2, 4), (3, 4))),
        "beam_offsets": place_ends(jax.random.randint(keys[1], (LEVELS, 2, 2, NB), -HALO, HALO - TAPS + 1), jax.random.fold_in(keys[1], 1), -HALO, HALO - TAPS).astype(jnp.int32),
        "range_offsets": place_ends(jax.random.randint(keys[2], (LEVELS, 2, 2, NB), -HALO, HALO), jax.random.fold_in(keys[2], 1), -HALO, HALO - 1).astype(jnp.int32),
        "beam_taps": jnp.clip(0.14941406 + 0.4482422 * jax.random.uniform(keys[3], (LEVELS, 2, 2, TAPS, NB), jnp.float32) ** steps_of(keys[3], (LEVELS, 2, 2, TAPS, NB), ((4, 4),), -0.2, 0.2), 0.14941406, 0.59765625).astype(jnp.bfloat16),
        "range_frac": jnp.clip(1.0 * jax.random.uniform(keys[4], (LEVELS, 2, 2, NB), jnp.float32) ** steps_of(keys[4], (LEVELS, 2, 2, NB), ((3, 4),), -0.2, 0.2), 0.0, 1.0),
        "phase_base": jnp.clip(jax.random.uniform(keys[5], (S, LEVELS, 2, NB), jnp.float32, -3.140625, 3.140625), -3.140625, 3.140625),
        "phase_rate": jnp.clip(jax.random.uniform(keys[6], (LEVELS, 2, NB), jnp.float32, -6.0, 6.0) * steps_of(keys[6], (LEVELS, 2, NB), ((2, 4),), -0.4, 0.0), -6.0, 6.0),
        "final_phase": jnp.clip(jax.random.uniform(keys[7], (S, NB), jnp.float32, -3.140625, 3.140625), -3.140625, 3.140625),
    }


def merge_one(blocks_in, level_idx, sub_index, beam_offsets, range_offsets, beam_taps, range_frac, phase_base, phase_rate):
    distance = S >> LEVELS - level_idx
    half_bit = sub_index // distance % 2
    first_sub = sub_index - half_bit * distance
    beam_ids = jnp.arange(NB, dtype=jnp.int32)
    range_ramp = jnp.arange(NR, dtype=jnp.int32).astype(jnp.float32) / NR - 0.5
    summed = jnp.zeros((2, NB, NR), jnp.float32)
    for child_idx in range(2):
        child_block = lax.dynamic_index_in_dim(blocks_in, (first_sub + child_idx * distance).astype(jnp.int32), 0, keepdims=False).astype(jnp.float32)
        padded = jnp.pad(child_block, ((0, 0), (HALO, HALO), (0, 0)))
        offsets = beam_offsets[level_idx, child_idx][half_bit]
        tap_weights = beam_taps[level_idx, child_idx][half_bit].astype(jnp.float32)
        interpolated = jnp.zeros((2, NB, NR), jnp.float32)
        for tap_idx in range(TAPS):
            row_ids = (beam_ids + HALO + offsets + tap_idx).astype(jnp.int32)
            interpolated = interpolated + tap_weights[tap_idx][None, :, None] * jnp.take(padded, row_ids, axis=1)
        range_shift = range_offsets[level_idx, child_idx][half_bit] + HALO
        fraction = range_frac[level_idx, child_idx][half_bit]
        widened = jnp.pad(interpolated, ((0, 0), (0, 0), (HALO, HALO)))
        shifted = jnp.zeros((2, NB, NR), jnp.float32)
        for offset_step in range(2 * HALO + 1):
            weight = jnp.where(range_shift == offset_step, 1.0 - fraction, 0.0) + jnp.where(range_shift + 1 == offset_step, fraction, 0.0)
            shifted = shifted + weight[None, :, None] * widened[:, :, offset_step:offset_step + NR]
        angles = phase_base[sub_index, level_idx, child_idx][:, None] + phase_rate[level_idx, child_idx][:, None] * range_ramp[None, :]
        cosine = jnp.cos(angles)
        sine_part = jnp.sin(angles)
        summed = summed + jnp.stack([cosine * shifted[0] - sine_part * shifted[1], sine_part * shifted[0] + cosine * shifted[1]])
    return summed.astype(jnp.bfloat16)

def reference(subimages, beam_offsets, range_offsets, beam_taps, range_frac, phase_base, phase_rate, final_phase):
    blocks = subimages
    for level_idx in range(LEVELS):
        blocks = lax.map(lambda sub_index: merge_one(blocks, level_idx, sub_index, beam_offsets, range_offsets, beam_taps, range_frac, phase_base, phase_rate), jnp.arange(S, dtype=jnp.int32))

    def accumulate(running, sub_index):
        child_block = blocks[sub_index].astype(jnp.float32)
        angles = final_phase[sub_index]
        cosine = jnp.cos(angles)[:, None]
        sine_part = jnp.sin(angles)[:, None]
        term = jnp.stack([cosine * child_block[0] - sine_part * child_block[1], sine_part * child_block[0] + cosine * child_block[1]])
        return (running + term, None)
    summed, unused = lax.scan(accumulate, jnp.zeros((2, NB, NR), jnp.float32), jnp.arange(S, dtype=jnp.int32))
    image = summed * (1.0 / math.sqrt(S))
    return image.reshape(2, N_ANG, B_DEV, NR)
```

```python
import functools
import math

import jax
import jax.numpy as jnp
from jax import lax
from jax.experimental import pallas as pl
from jax.experimental.pallas import tpu as pltpu
from jax.sharding import PartitionSpec as P

MESH = pl.DeviceIdType.MESH
F32 = jnp.float32
BF16 = jnp.bfloat16
I32 = jnp.int32

ROWS_BELOW_IN = (16, 8, 4)
ROWS_BELOW_OUT = (8, 4, 0)
ROWS_IN = (160, 144, 144)
ROWS_OUT = (144, 144, 128)
NT = (((1,), (1,)), ((), ()))

SIN_C = (0.9999999957158404, -0.16666657969904627, 0.008333050617327633, -0.0001980904635743576, 2.605166275944652e-06)
COS_C = (0.9999999997799074, -0.49999999356956554, 0.04166663620892635, -0.0013888360842520568, 2.4760135515714637e-05, -2.605107635999247e-07)


def cos_sin(angle):
    turns = jnp.floor(angle * (0.5 / math.pi) + 0.5)
    rest = (angle - turns * 6.28125) - turns * (2 * math.pi - 6.28125)
    half = 0.5 * rest
    sq = half * half
    s = jnp.full_like(sq, SIN_C[-1])
    for coef in SIN_C[-2::-1]:
        s = s * sq + coef
    s = s * half
    c = jnp.full_like(sq, COS_C[-1])
    for coef in COS_C[-2::-1]:
        c = c * sq + coef
    return 1.0 - 2.0 * s * s, 2.0 * s * c


def lane_of(shape):
    return lax.broadcasted_iota(I32, shape, len(shape) - 1)


def row_of(shape):
    return lax.broadcasted_iota(I32, shape, len(shape) - 2)


def dot(a, b):
    return jnp.dot(a, b, preferred_element_type=F32)


def shift_rows(range_offset, fraction):
    o = range_offset + 4.0
    b4 = jnp.where(o >= 4.0, 1.0, 0.0)
    o = o - 4.0 * b4
    b2 = jnp.where(o >= 2.0, 1.0, 0.0)
    b1 = o - 2.0 * b2
    return b4, b2, (1.0 - b1) * (1.0 - fraction), (1.0 - b1) * fraction + b1 * (1.0 - fraction), b1 * fraction


def tap_matrix(lag, taps):
    out = jnp.where(lag == 3.0, taps[3], 0.0)
    for t in (2, 1, 0):
        out = jnp.where(lag == float(t), taps[t], out)
    return out


def kernel(
    sub, bo, ro, bt, rf, pb, pr, fp, out,
    XM, PE, PH, TAB, TABH, PS, PB2, PB1, PB0, PB1H, PB0H,
    RHS, RHSH0, RHSH1, WT, WTH, EM, EH, PC2, PC1, PC0, PCH,
    L0, L1, L2, IB, IH, S2, S2H, HB, ACC, FB, SB, RS,
    ssem, rsem, rs_ssem, rs_rsem,
):
    A = lax.axis_index("aper")
    X = lax.axis_index("rng")
    Y = lax.axis_index("ang")
    top = A // 4
    low = A % 4
    c2 = top // 4
    c1 = (top // 2) % 2
    c0 = top % 2
    cbits = (c0, c1, c2)
    t2 = c2
    t10 = top % 4

    barrier = pltpu.get_barrier_semaphore()

    def tell(**where):
        pl.semaphore_signal(barrier, inc=1, device_id=where, device_id_type=MESH)

    def tell_aper(k, carry):
        tell(aper=(A + k) % 32)
        return carry

    lax.fori_loop(1, 32, tell_aper, 0)
    y_ok = (Y > 0, Y < 3)
    x_ok = (X > 0, X < 3)
    for dy, ok_y in ((-1, y_ok[0]), (1, y_ok[1])):
        @pl.when(ok_y)
        def _():
            for q in range(4):
                tell(aper=4 * (t2 * 4 + q) + low, ang=Y + dy)
    for dx, ok_x in ((-1, x_ok[0]), (1, x_ok[1])):
        @pl.when(ok_x)
        def _():
            tell(rng=X + dx)
        for dy, ok_y in ((-1, y_ok[0]), (1, y_ok[1])):
            @pl.when(jnp.logical_and(ok_x, ok_y))
            def _():
                tell(rng=X + dx, ang=Y + dy)
    one = lambda ok: jnp.where(ok, 1, 0).astype(I32)
    ny = one(y_ok[0]) + one(y_ok[1])
    nx = one(x_ok[0]) + one(x_ok[1])

    eye = jnp.where(row_of((128, 128)) == lane_of((128, 128)), 1.0, 0.0).astype(BF16)
    for j in range(4):
        for ri in range(2):
            turned = lax.dot_general(eye, sub[j, ri], NT, preferred_element_type=F32).astype(BF16)
            XM[2 * j + ri, 0, 16:144, :] = turned[:, 0:128]
            XM[2 * j + ri, 1, 16:144, :] = turned[:, 128:256]
    for side, first in ((0, 0), (1, 240)):
        edge = sub[:, :, first:first + 16, :].reshape(128, 128)
        PE[side] = lax.dot_general(eye, edge, NT, preferred_element_type=F32).astype(BF16)

    for lvl in range(3):
        c = cbits[lvl]
        offs = bo[lvl, c].astype(F32)
        rofs = ro[lvl, c].astype(F32)
        frac = rf[lvl, c]
        taps = bt[lvl, c].astype(F32)
        rates = pr[lvl]
        rate = jnp.where(c == 0, rates[0:1], rates[1:2])
        for b in range(2):
            cut = slice(128 * b, 128 * b + 128)
            r0 = 16 * lvl
            TAB[b, r0:r0 + 2, :] = offs[:, cut]
            TAB[b, r0 + 2:r0 + 4, :] = rofs[:, cut]
            TAB[b, r0 + 4:r0 + 6, :] = frac[:, cut]
            TAB[b, r0 + 6:r0 + 7, :] = rate[:, cut]
            TAB[b, r0 + 7:r0 + 8, :] = rate[:, cut]
            TAB[b, r0 + 8:r0 + 12, :] = taps[0, :, cut]
            TAB[b, r0 + 12:r0 + 16, :] = taps[1, :, cut]
    for j in range(4):
        for lvl in range(3):
            base = pb[j, lvl]
            for c in range(2):
                for b in range(2):
                    PS[lvl, c, b, j:j + 1, :] = base[c:c + 1, 128 * b:128 * b + 128]
    PB2[top] = PS[2, c2]
    PB1[t10] = PS[1, c1]
    PB0[c0] = PS[0, c0]
    SHARED = 32

    @pl.when(X == 0)
    def _():
        XM[:, :, 0:16, :] = jnp.zeros((8, 2, 16, 128), BF16)
        PH[:, 0:16, :] = jnp.zeros((2, 16, 128), BF16)

    @pl.when(X == 3)
    def _():
        XM[:, :, 144:160, :] = jnp.zeros((8, 2, 16, 128), BF16)
        PH[:, 144:160, :] = jnp.zeros((2, 16, 128), BF16)

    for side, edge_at in ((0, 0), (1, 3)):
        @pl.when(Y == edge_at)
        def _():
            PH[side] = jnp.zeros((160, 128), BF16)
            TABH[side] = jnp.zeros((SHARED, 128), F32)
            PB1H[side] = jnp.zeros((4, 4, 128), F32)
            PB0H[side] = jnp.zeros((2, 4, 128), F32)

    copies = []
    count = [0]

    def plan(src, dst, slot, send_if, take_if, **where):
        copies.append((
            send_if, take_if,
            pltpu.make_async_remote_copy(
                src_ref=src, dst_ref=dst, send_sem=ssem.at[count[0]], recv_sem=rsem.at[slot],
                device_id=where, device_id_type=MESH,
            ),
        ))
        count[0] += 1

    plan(XM.at[:, :, pl.ds(128, 16), :], XM.at[:, :, pl.ds(0, 16), :], 0, x_ok[1], x_ok[0], rng=X + 1)
    plan(XM.at[:, :, pl.ds(16, 16), :], XM.at[:, :, pl.ds(144, 16), :], 1, x_ok[0], x_ok[1], rng=X - 1)
    both = jnp.logical_and
    for side in range(2):
        dy = 1 - 2 * side
        send_y, take_y = y_ok[1 - side], y_ok[side]
        edge = PE.at[1 - side]
        plan(edge, PH.at[side, pl.ds(16, 128), :], 2 + side, send_y, take_y, ang=Y + dy)
        plan(edge.at[pl.ds(112, 16), :], PH.at[side, pl.ds(0, 16), :], 4 + side,
             both(send_y, x_ok[1]), both(take_y, x_ok[0]), rng=X + 1, ang=Y + dy)
        plan(edge.at[pl.ds(0, 16), :], PH.at[side, pl.ds(144, 16), :], 6 + side,
             both(send_y, x_ok[0]), both(take_y, x_ok[1]), rng=X - 1, ang=Y + dy)
        plan(TAB.at[1 - side, pl.ds(0, SHARED), :], TABH.at[side], 8 + side, send_y, take_y, ang=Y + dy)
    sends = []
    takes = []

    def plan_send(src, dst, slot, send_if, **where):
        sends.append((send_if, pltpu.make_async_remote_copy(
            src_ref=src, dst_ref=dst, send_sem=ssem.at[count[0]], recv_sem=rsem.at[slot],
            device_id=where, device_id_type=MESH)))
        count[0] += 1

    def plan_take(dst, slot, take_if):
        takes.append((take_if, pltpu.make_async_remote_copy(
            src_ref=dst, dst_ref=dst, send_sem=ssem.at[0], recv_sem=rsem.at[slot],
            device_id=dict(aper=(A + 1) % 32), device_id_type=MESH)))

    for e in range(2):
        plan_send(PS.at[0, e], PB0.at[c0], 22 + c0, c0 != e, aper=4 * (2 * (top // 2) + e) + low)
        plan_take(PB0.at[e], 22 + e, c0 != e)
        for side in range(2):
            plan_send(PS.at[0, e, 1 - side], PB0H.at[side, c0], 32 + 2 * side + c0, y_ok[1 - side],
                      aper=4 * (2 * (top // 2) + e) + low, ang=Y + 1 - 2 * side)
            plan_take(PB0H.at[side, e], 32 + 2 * side + e, y_ok[side])
    for q in range(4):
        plan_send(PS.at[1, q // 2], PB1.at[t10], 18 + t10, t10 != q, aper=4 * (t2 * 4 + q) + low)
        plan_take(PB1.at[q], 18 + q, t10 != q)
        for side in range(2):
            plan_send(PS.at[1, q // 2, 1 - side], PB1H.at[side, t10], 24 + 4 * side + t10, y_ok[1 - side],
                      aper=4 * (t2 * 4 + q) + low, ang=Y + 1 - 2 * side)
            plan_take(PB1H.at[side, q], 24 + 4 * side + q, y_ok[side])
    for t in range(8):
        plan_send(PS.at[2, t // 4], PB2.at[top], 10 + top, top != t, aper=4 * t + low)
        plan_take(PB2.at[t], 10 + t, top != t)

    pl.semaphore_wait(barrier, 31 + 4 * ny + nx + nx * ny)
    for send_if, _, copy in copies:
        pl.when(send_if)(copy.start)
    for send_if, copy in sends:
        pl.when(send_if)(copy.start)

    k_at = row_of((256, 128))
    near = (jnp.where(k_at < 192, k_at, k_at - 256) - lane_of((256, 128))).astype(F32)
    for lvl in range(3):
        r0 = 16 * lvl
        for b in range(2):
            for h in range(2):
                lag = near - TAB[b, r0 + h:r0 + h + 1, :]
                taps = [TAB[b, r0 + 8 + 4 * h + t:r0 + 9 + 4 * h + t, :] for t in range(4)]
                RHS[lvl, b, :, 128 * h:128 * h + 128] = tap_matrix(lag, taps).astype(BF16)
                rows = shift_rows(TAB[b, r0 + 2 + h:r0 + 3 + h, :], TAB[b, r0 + 4 + h:r0 + 5 + h, :])
                for k, row in enumerate(rows):
                    WT[lvl, h, b, k:k + 1, :] = row

    def ramp_of(first, lvl):
        at = X * 128 - ROWS_BELOW_OUT[lvl] + first + row_of((16, 128))
        inside = jnp.logical_and(at >= 0, at < 512)
        return at.astype(F32) * (1.0 / 512) - 0.5, inside

    def swing(i, carry):
        first = pl.multiple_of(i * 16, 16)
        for lvl in range(3):
            ramp, inside = ramp_of(first, lvl)
            for b in range(2):
                cs = cos_sin(ramp * TAB[b, 16 * lvl + 6:16 * lvl + 7, :])
                for k in range(2):
                    EM[lvl, b, k, pl.ds(first, 16), :] = jnp.where(inside, cs[k], 0.0)
        return carry

    lax.fori_loop(0, 9, swing, 0)

    for _, take_if, copy in copies:
        pl.when(take_if)(copy.wait_recv)
    for take_if, copy in takes:
        pl.when(take_if)(copy.wait_recv)

    for h0 in range(2):
        for b in range(2):
            cs = cos_sin(PB0[h0, b])
            PC0[h0, b, 0], PC0[h0, b, 1] = cs
    for q in range(4):
        for b in range(2):
            cs = cos_sin(PB1[q, b])
            PC1[q, b, 0], PC1[q, b, 1] = cs
    for t in range(8):
        group = fp[16 * t:16 * t + 16, :]
        mine = group[0:4]
        for k in range(1, 4):
            mine = jnp.where(low == k, group[4 * k:4 * k + 4], mine)
        for b in range(2):
            cs = cos_sin(PB2[t, b] + mine[:, 128 * b:128 * b + 128])
            PC2[t, b, 0], PC2[t, b, 1] = cs

    lane1 = lane_of((1, 128))
    k_q = jnp.where(k_at < 64, 256 + k_at, jnp.where(k_at < 192, k_at - 128, k_at))

    def packed(lo, hi, width):
        half = width // 2
        lane = lane_of(lo.shape)
        got = jnp.where(lane < half, pltpu.roll(lo, half, 1), pltpu.roll(hi, half, 1))
        got = jnp.where(lane < width, got, 0.0)
        step = width
        while step < 128:
            got = got + pltpu.roll(got, step, 1)
            step *= 2
        return got

    for lvl in range(2):
        width = 16 >> lvl
        half = width // 2
        r0 = 16 * lvl
        tab = packed(TABH[0, r0:r0 + 16, :], TABH[1, r0:r0 + 16, :], width)

        def pick(first, second):
            return jnp.where(lane1 < 64, tab[first:first + 1], tab[second:second + 1])

        within = lane1 % width
        beam = jnp.where(within < half, within - half, 256 + within - half)
        lag = (k_q - beam).astype(F32) - pick(0, 1)
        full = tap_matrix(lag, [pick(8 + t, 12 + t) for t in range(4)])
        source = (lane1 // width) % (4 << lvl)
        dest = RHSH0 if lvl == 0 else RHSH1
        for m in range(4 << lvl):
            dest[m] = jnp.where(source == m, full, 0.0).astype(BF16)
        for k, row in enumerate(shift_rows(pick(2, 3), pick(4, 5))):
            WTH[lvl, k:k + 1, :] = row
        known = jnp.where(within < half, one(y_ok[0]), one(y_ok[1])) > 0

        def swing_halo(i, carry, lvl=lvl, rate=tab[6:7], known=known):
            first = pl.multiple_of(i * 16, 16)
            ramp, inside = ramp_of(first, lvl)
            cs = cos_sin(ramp * rate)
            ok = jnp.logical_and(inside, known)
            for k in range(2):
                EH[lvl, k, pl.ds(first, 16), :] = jnp.where(ok, cs[k], 0.0)
            return carry

        lax.fori_loop(0, 9, swing_halo, 0)
        owner = lane1 // width
        total = jnp.zeros((1, 128), F32)
        for q in range(2 << lvl):
            lo, hi = (PB0H[0, q], PB0H[1, q]) if lvl == 0 else (PB1H[0, q], PB1H[1, q])
            rows = packed(lo, hi, width)
            mine = 4 * q + row_of((4, 128)) == owner
            total = total + jnp.sum(jnp.where(mine, rows, 0.0), axis=0, keepdims=True)
        cs = cos_sin(total)
        for k in range(2):
            PCH[lvl, k, 0:1, :] = cs[k]

    left_half = lane_of((16, 128)) < 64

    def lay(dest, m, row, main0, main1, halo, beyond):
        dest[m, 0, pl.ds(row, 16), 0:128] = main0
        dest[m, 0, pl.ds(row, 16), 128:256] = jnp.where(left_half, main1, halo)
        dest[m, 1, pl.ds(row, 16), 0:128] = main1
        dest[m, 1, pl.ds(row, 16), 128:256] = jnp.where(left_half, halo, main0)
        if beyond:
            dest[m, 2, pl.ds(row, 16), 0:128] = halo
            dest[m, 2, pl.ds(row, 16), 128:256] = jnp.where(left_half, main0, main1)

    for j in range(4):
        for ri in range(2):
            img = 2 * j + ri
            for first in range(0, 160, 16):
                lo = pltpu.roll(PH[0, first:first + 16, :].astype(F32), (128 - 16 * img - 16) % 128, 1)
                hi = pltpu.roll(PH[1, first:first + 16, :].astype(F32), (128 - 16 * img) % 128, 1)
                halo = jnp.where(left_half, hi, lo).astype(BF16)
                lay(L0, j, 160 * ri + first, XM[img, 0, first:first + 16, :], XM[img, 1, first:first + 16, :], halo, True)

    def settle(src, at, dst, to, b4, b2, lvl, rows):
        d = ROWS_BELOW_IN[lvl] - ROWS_BELOW_OUT[lvl]
        for first in range(0, rows, 8):
            a, b, c, e = (src[at + (pl.ds(first + d + o, 8), slice(None))] for o in (-4, -2, 0, 2))
            dst[to + (pl.ds(first, 8), slice(None))] = jnp.where(b2, jnp.where(b4, e, b), jnp.where(b4, c, a))

    def three(src, at, first, w):
        return (
            w[0] * src[at + (pl.ds(first, 16), slice(None))]
            + w[1] * src[at + (pl.ds(first + 1, 16), slice(None))]
            + w[2] * src[at + (pl.ds(first + 2, 16), slice(None))]
        )

    def turn(re, im, c, s):
        return re * c - im * s, re * s + im * c

    for lvl in range(2):
        src, dst, tail = (L0, L1, RHSH0) if lvl == 0 else (L1, L2, RHSH1)
        rows = ROWS_IN[lvl]
        images = 4 << lvl
        width = 16 >> lvl
        phases = PC0 if lvl == 0 else PC1

        got = dot(src[0, 2], tail[0])
        for m in range(1, images):
            got = got + dot(src[m, 2], tail[m])
        for ri in range(2):
            IH[ri, 0:rows, :] = got[rows * ri:rows * ri + rows]
            settle(IH, (ri,), S2H, (ri,), WTH[lvl, 0:1, :] > 0.5, WTH[lvl, 1:2, :] > 0.5, lvl, 152)
        w = [WTH[lvl, k:k + 1, :] for k in (2, 3, 4)]
        for first in range(0, 144, 16):
            re, im = three(S2H, (0,), first, w), three(S2H, (1,), first, w)
            re, im = turn(re, im, EH[lvl, 0, first:first + 16, :], EH[lvl, 1, first:first + 16, :])
            re, im = turn(re, im, PCH[lvl, 0, 0:1, :], PCH[lvl, 1, 0:1, :])
            HB[0, first:first + 16, :] = re
            HB[1, first:first + 16, :] = im

        def image(m, carry, lvl=lvl, src=src, dst=dst, rows=rows, images=images, width=width, phases=phases):
            q = m // 4
            j = m % 4
            for b in range(2):
                got = dot(src[m, b], RHS[lvl, b])
                for h in range(2):
                    for ri in range(2):
                        IB[b, h, ri, 0:rows, :] = got[rows * ri:rows * ri + rows, 128 * h:128 * h + 128]
            for h in range(2):
                idx = images * h + m
                for b in range(2):
                    b4 = WT[lvl, h, b, 0:1, :] > 0.5
                    b2 = WT[lvl, h, b, 1:2, :] > 0.5
                    for ri in range(2):
                        settle(IB, (b, h, ri), S2, (h, b, ri), b4, b2, lvl, 152)
                w = [[WT[lvl, h, b, k:k + 1, :] for k in (2, 3, 4)] for b in range(2)]
                who = h if lvl == 0 else 2 * h + q
                turned = [[phases[who, b, k, pl.ds(j, 1), :] for k in range(2)] for b in range(2)]
                back = 128 - (width * idx + width // 2)
                for first in range(0, 144, 16):
                    main = []
                    for b in range(2):
                        re, im = three(S2, (h, b, 0), first, w[b]), three(S2, (h, b, 1), first, w[b])
                        re, im = turn(re, im, EM[lvl, b, 0, first:first + 16, :], EM[lvl, b, 1, first:first + 16, :])
                        main.append(turn(re, im, turned[b][0], turned[b][1]))
                    for ri in range(2):
                        halo = pltpu.roll(HB[ri, first:first + 16, :], back, 1).astype(BF16)
                        lay(dst, idx, 144 * ri + first, main[0][ri].astype(BF16), main[1][ri].astype(BF16), halo, lvl == 0)
            return carry

        lax.fori_loop(0, images, image, 0)

    def rs_copy(k):
        return pltpu.make_async_remote_copy(
            src_ref=SB.at[k], dst_ref=RS.at[A], send_sem=rs_ssem.at[k], recv_sem=rs_rsem.at[A],
            device_id=dict(aper=k), device_id_type=MESH)

    for b in range(2):
        ACC[...] = jnp.zeros((2, 2, 144, 128), F32)

        def gather(n, carry, b=b):
            got = dot(L2[n, b], RHS[2, b])
            for h in range(2):
                t = 4 * h + n // 4
                c = PC2[t, b, 0, pl.ds(n % 4, 1), :]
                s = PC2[t, b, 1, pl.ds(n % 4, 1), :]
                for first in range(0, 136, 8):
                    re = got[first:first + 8, 128 * h:128 * h + 128]
                    im = got[144 + first:152 + first, 128 * h:128 * h + 128]
                    re, im = turn(re, im, c, s)
                    ACC[h, 0, first:first + 8, :] += re
                    ACC[h, 1, first:first + 8, :] += im
            return carry

        lax.fori_loop(0, 16, gather, 0)
        for h in range(2):
            b4 = WT[2, h, b, 0:1, :] > 0.5
            b2 = WT[2, h, b, 1:2, :] > 0.5
            for ri in range(2):
                settle(ACC, (h, ri), S2, (h, b, ri), b4, b2, 2, 136)
        w = [[WT[2, h, b, k:k + 1, :] for k in (2, 3, 4)] for h in range(2)]
        for first in range(0, 128, 16):
            re = three(S2, (0, b, 0), first, w[0]) + three(S2, (1, b, 0), first, w[1])
            im = three(S2, (0, b, 1), first, w[0]) + three(S2, (1, b, 1), first, w[1])
            re, im = turn(re, im, EM[2, b, 0, first:first + 16, :], EM[2, b, 1, first:first + 16, :])
            FB[0, first:first + 16, :] = re.astype(BF16)
            FB[1, first:first + 16, :] = im.astype(BF16)
        parts = [lax.dot_general(eye, FB[ri], NT, preferred_element_type=F32).reshape(16, 8, 128) for ri in range(2)]
        SB[16 * b:16 * b + 16] = jnp.concatenate(parts, axis=1).astype(BF16)

        def send(k, carry):
            @pl.when(k != A)
            def _():
                rs_copy(k).start()
            return carry

        lax.fori_loop(16 * b, 16 * b + 16, send, 0)

    RS[A] = SB[A]

    def arrive(k, total):
        @pl.when(k != A)
        def _():
            pltpu.make_async_remote_copy(
                src_ref=SB.at[k], dst_ref=RS.at[k], send_sem=rs_ssem.at[k], recv_sem=rs_rsem.at[k],
                device_id=dict(aper=k), device_id_type=MESH).wait_recv()
        return total + RS[k].astype(F32)

    total = lax.fori_loop(0, 32, arrive, jnp.zeros((16, 128), F32)) * (1.0 / math.sqrt(128.0))
    out[0, 0] = total[0:8]
    out[1, 0] = total[8:16]

    for send_if, _, copy in copies:
        pl.when(send_if)(copy.wait_send)
    for send_if, copy in sends:
        pl.when(send_if)(copy.wait_send)

    def sent(k, carry):
        @pl.when(k != A)
        def _():
            rs_copy(k).wait_send()
        return carry

    lax.fori_loop(0, 32, sent, 0)


def body(*args):
    v = pltpu.VMEM
    return pl.pallas_call(
        kernel,
        out_shape=jax.ShapeDtypeStruct((2, 1, 8, 128), F32),
        in_specs=[pl.BlockSpec(memory_space=pltpu.VMEM)] * 8,
        out_specs=pl.BlockSpec(memory_space=pltpu.VMEM),
        scratch_shapes=[
            v((8, 2, 160, 128), BF16),
            v((2, 128, 128), BF16),
            v((2, 160, 128), BF16),
            v((2, 48, 128), F32),
            v((2, 32, 128), F32),
            v((3, 2, 2, 4, 128), F32),
            v((8, 2, 4, 128), F32),
            v((4, 2, 4, 128), F32),
            v((2, 2, 4, 128), F32),
            v((2, 4, 4, 128), F32),
            v((2, 2, 4, 128), F32),
            v((3, 2, 256, 256), BF16),
            v((4, 256, 128), BF16),
            v((8, 256, 128), BF16),
            v((3, 2, 2, 8, 128), F32),
            v((2, 8, 128), F32),
            v((3, 2, 2, 144, 128), F32),
            v((2, 2, 144, 128), F32),
            v((8, 2, 2, 4, 128), F32),
            v((4, 2, 2, 4, 128), F32),
            v((2, 2, 2, 4, 128), F32),
            v((2, 2, 8, 128), F32),
            v((4, 3, 320, 256), BF16),
            v((8, 3, 288, 256), BF16),
            v((16, 2, 288, 256), BF16),
            v((2, 2, 2, 176, 128), F32),
            v((2, 176, 128), F32),
            v((2, 2, 2, 160, 128), F32),
            v((2, 160, 128), F32),
            v((2, 144, 128), F32),
            v((2, 2, 144, 128), F32),
            v((2, 128, 128), BF16),
            v((32, 16, 128), BF16),
            v((32, 16, 128), BF16),
            pltpu.SemaphoreType.DMA((48,)),
            pltpu.SemaphoreType.DMA((48,)),
            pltpu.SemaphoreType.DMA((32,)),
            pltpu.SemaphoreType.DMA((32,)),
        ],
        compiler_params=pltpu.CompilerParams(collective_id=0, has_side_effects=True, vmem_limit_bytes=48 * 1024 * 1024),
    )(*args)


def solution(mesh):
    in_specs = (
        P("aper", None, "ang", "rng"),
        P(None, None, None, "ang"),
        P(None, None, None, "ang"),
        P(None, None, None, None, "ang"),
        P(None, None, None, "ang"),
        P("aper", None, None, "ang"),
        P(None, None, "ang"),
        P(None, "ang"),
    )
    out_specs = P(None, "ang", "aper", "rng")
    return jax.shard_map(body, mesh=mesh, in_specs=in_specs, out_specs=out_specs, check_vma=False)
```

```python
import functools
import math

import jax
import jax.numpy as jnp
from jax import lax
from jax.experimental import pallas as pl
from jax.experimental.pallas import tpu as pltpu
from jax.sharding import PartitionSpec as P

MESH = pl.DeviceIdType.MESH
F32 = jnp.float32
BF16 = jnp.bfloat16
I32 = jnp.int32

ROWS_BELOW_IN = (16, 8, 4)
ROWS_BELOW_OUT = (8, 4, 0)
ROWS_IN = (160, 144, 144)
ROWS_OUT = (144, 144, 128)
NT = (((1,), (1,)), ((), ()))

SIN_C = (0.9999999957158404, -0.16666657969904627, 0.008333050617327633, -0.0001980904635743576, 2.605166275944652e-06)
COS_C = (0.9999999997799074, -0.49999999356956554, 0.04166663620892635, -0.0013888360842520568, 2.4760135515714637e-05, -2.605107635999247e-07)


def cos_sin(angle):
    turns = jnp.floor(angle * (0.5 / math.pi) + 0.5)
    rest = (angle - turns * 6.28125) - turns * (2 * math.pi - 6.28125)
    half = 0.5 * rest
    sq = half * half
    s = jnp.full_like(sq, SIN_C[-1])
    for coef in SIN_C[-2::-1]:
        s = s * sq + coef
    s = s * half
    c = jnp.full_like(sq, COS_C[-1])
    for coef in COS_C[-2::-1]:
        c = c * sq + coef
    return 1.0 - 2.0 * s * s, 2.0 * s * c


def lane_of(shape):
    return lax.broadcasted_iota(I32, shape, len(shape) - 1)


def row_of(shape):
    return lax.broadcasted_iota(I32, shape, len(shape) - 2)


def dot(a, b):
    return jnp.dot(a, b, preferred_element_type=F32)


def shift_rows(range_offset, fraction):
    o = range_offset + 4.0
    b4 = jnp.where(o >= 4.0, 1.0, 0.0)
    o = o - 4.0 * b4
    b2 = jnp.where(o >= 2.0, 1.0, 0.0)
    b1 = o - 2.0 * b2
    return b4, b2, (1.0 - b1) * (1.0 - fraction), (1.0 - b1) * fraction + b1 * (1.0 - fraction), b1 * fraction


def tap_matrix(lag, taps):
    out = jnp.where(lag == 3.0, taps[3], 0.0)
    for t in (2, 1, 0):
        out = jnp.where(lag == float(t), taps[t], out)
    return out


def kernel(
    *refs,
):
    ins, rest = refs[:8], refs[8:]
    out = rest[0]
    here = rest[1:9]
    in_sem = rest[9]
    (sub, bo, ro, bt, rf, pb, pr, fp) = here
    (
    XS, XR, PE, PH, TAB, TABH, PS, PB2, PB1, PB0, PB1H, PB0H,
    RHS, RHSH0, RHSH1, WT, WTH, EM, EH, PC2, PC1, PC0, PCH,
    L0, L1, L2, IB, IH, S2, S2H, HB, ACC, FB, SB, RS,
    ssem, rsem, rs_ssem, rs_rsem,
    ) = rest[10:]
    loads = [pltpu.make_async_copy(ins[k], here[k], in_sem.at[k]) for k in (5, 0, 1, 2, 3, 4, 6, 7)]
    for load in loads:
        load.start()
    A = lax.axis_index("aper")
    X = lax.axis_index("rng")
    Y = lax.axis_index("ang")
    top = A // 4
    low = A % 4
    c2 = top // 4
    c1 = (top // 2) % 2
    c0 = top % 2
    cbits = (c0, c1, c2)
    t2 = c2
    t10 = top % 4

    barrier = pltpu.get_barrier_semaphore()

    def tell(**where):
        pl.semaphore_signal(barrier, inc=1, device_id=where, device_id_type=MESH)

    def tell_aper(k, carry):
        tell(aper=(A + k) % 32)
        return carry

    lax.fori_loop(1, 32, tell_aper, 0)
    y_ok = (Y > 0, Y < 3)
    x_ok = (X > 0, X < 3)
    for dy, ok_y in ((-1, y_ok[0]), (1, y_ok[1])):
        @pl.when(ok_y)
        def _():
            for q in range(4):
                tell(aper=4 * (t2 * 4 + q) + low, ang=Y + dy)
    for dx, ok_x in ((-1, x_ok[0]), (1, x_ok[1])):
        @pl.when(ok_x)
        def _():
            tell(rng=X + dx)
        for dy, ok_y in ((-1, y_ok[0]), (1, y_ok[1])):
            @pl.when(jnp.logical_and(ok_x, ok_y))
            def _():
                tell(rng=X + dx, ang=Y + dy)
    one = lambda ok: jnp.where(ok, 1, 0).astype(I32)
    ny = one(y_ok[0]) + one(y_ok[1])
    nx = one(x_ok[0]) + one(x_ok[1])

    for load in loads:
        load.wait()

    eye = jnp.where(row_of((128, 128)) == lane_of((128, 128)), 1.0, 0.0).astype(BF16)
    for j in range(4):
        for ri in range(2):
            turned = lax.dot_general(eye, sub[j, ri], NT, preferred_element_type=F32).astype(BF16)
            for b in range(2):
                main = turned[:, 128 * b:128 * b + 128]
                L0[b, 320 * j + 160 * ri + 16:320 * j + 160 * ri + 144, 0:128] = main
                XS[2 * j + ri, b, 0] = main[0:16]
                XS[2 * j + ri, b, 1] = main[112:128]
    for side, first in ((0, 0), (1, 240)):
        edge = sub[:, :, first:first + 16, :].reshape(128, 128)
        PE[side] = lax.dot_general(eye, edge, NT, preferred_element_type=F32).astype(BF16)

    for lvl in range(3):
        c = cbits[lvl]
        offs = bo[lvl, c].astype(F32)
        rofs = ro[lvl, c].astype(F32)
        frac = rf[lvl, c]
        taps = bt[lvl, c].astype(F32)
        rates = pr[lvl]
        rate = jnp.where(c == 0, rates[0:1], rates[1:2])
        for b in range(2):
            cut = slice(128 * b, 128 * b + 128)
            r0 = 16 * lvl
            TAB[b, r0:r0 + 2, :] = offs[:, cut]
            TAB[b, r0 + 2:r0 + 4, :] = rofs[:, cut]
            TAB[b, r0 + 4:r0 + 6, :] = frac[:, cut]
            TAB[b, r0 + 6:r0 + 7, :] = rate[:, cut]
            TAB[b, r0 + 7:r0 + 8, :] = rate[:, cut]
            TAB[b, r0 + 8:r0 + 12, :] = taps[0, :, cut]
            TAB[b, r0 + 12:r0 + 16, :] = taps[1, :, cut]
    for j in range(4):
        for lvl in range(3):
            base = pb[j, lvl]
            for c in range(2):
                for b in range(2):
                    PS[lvl, c, b, j:j + 1, :] = base[c:c + 1, 128 * b:128 * b + 128]
    PB2[top] = PS[2, c2]
    PB1[t10] = PS[1, c1]
    PB0[c0] = PS[0, c0]
    SHARED = 32

    @pl.when(X == 0)
    def _():
        XR[:, :, 0] = jnp.zeros((8, 2, 16, 128), BF16)
        PH[:, 0:16, :] = jnp.zeros((2, 16, 128), BF16)

    @pl.when(X == 3)
    def _():
        XR[:, :, 1] = jnp.zeros((8, 2, 16, 128), BF16)
        PH[:, 144:160, :] = jnp.zeros((2, 16, 128), BF16)

    for side, edge_at in ((0, 0), (1, 3)):
        @pl.when(Y == edge_at)
        def _():
            PH[side] = jnp.zeros((160, 128), BF16)
            TABH[side] = jnp.zeros((SHARED, 128), F32)
            PB1H[side] = jnp.zeros((4, 4, 128), F32)
            PB0H[side] = jnp.zeros((2, 4, 128), F32)

    k_at = row_of((256, 128))
    near = (jnp.where(k_at < 192, k_at, k_at - 256) - lane_of((256, 128))).astype(F32)
    for lvl in range(3):
        r0 = 16 * lvl
        for b in range(2):
            for h in range(2):
                lag = near - TAB[b, r0 + h:r0 + h + 1, :]
                taps = [TAB[b, r0 + 8 + 4 * h + t:r0 + 9 + 4 * h + t, :] for t in range(4)]
                RHS[lvl, b, :, 128 * h:128 * h + 128] = tap_matrix(lag, taps).astype(BF16)
                rows = shift_rows(TAB[b, r0 + 2 + h:r0 + 3 + h, :], TAB[b, r0 + 4 + h:r0 + 5 + h, :])
                for k, row in enumerate(rows):
                    WT[lvl, h, b, k:k + 1, :] = row

    def ramp_of(first, lvl):
        at = X * 128 - ROWS_BELOW_OUT[lvl] + first + row_of((16, 128))
        inside = jnp.logical_and(at >= 0, at < 512)
        return at.astype(F32) * (1.0 / 512) - 0.5, inside

    def swing(i, carry):
        first = pl.multiple_of(i * 16, 16)
        for lvl in range(3):
            ramp, inside = ramp_of(first, lvl)
            for b in range(2):
                cs = cos_sin(ramp * TAB[b, 16 * lvl + 6:16 * lvl + 7, :])
                for k in range(2):
                    EM[lvl, b, k, pl.ds(first, 16), :] = jnp.where(inside, cs[k], 0.0)
        return carry

    lax.fori_loop(0, 9, swing, 0)

    copies = []
    count = [0]

    def plan(src, dst, slot, send_if, take_if, **where):
        copies.append((
            send_if, take_if,
            pltpu.make_async_remote_copy(
                src_ref=src, dst_ref=dst, send_sem=ssem.at[count[0]], recv_sem=rsem.at[slot],
                device_id=where, device_id_type=MESH,
            ),
        ))
        count[0] += 1

    plan(XS.at[:, :, 1], XR.at[:, :, 0], 0, x_ok[1], x_ok[0], rng=X + 1)
    plan(XS.at[:, :, 0], XR.at[:, :, 1], 1, x_ok[0], x_ok[1], rng=X - 1)
    both = jnp.logical_and
    for side in range(2):
        dy = 1 - 2 * side
        send_y, take_y = y_ok[1 - side], y_ok[side]
        edge = PE.at[1 - side]
        plan(edge, PH.at[side, pl.ds(16, 128), :], 2 + side, send_y, take_y, ang=Y + dy)
        plan(edge.at[pl.ds(112, 16), :], PH.at[side, pl.ds(0, 16), :], 4 + side,
             both(send_y, x_ok[1]), both(take_y, x_ok[0]), rng=X + 1, ang=Y + dy)
        plan(edge.at[pl.ds(0, 16), :], PH.at[side, pl.ds(144, 16), :], 6 + side,
             both(send_y, x_ok[0]), both(take_y, x_ok[1]), rng=X - 1, ang=Y + dy)
        plan(TAB.at[1 - side, pl.ds(0, SHARED), :], TABH.at[side], 8 + side, send_y, take_y, ang=Y + dy)
    sends = []
    takes = ([], [], [])

    def plan_send(src, dst, slot, send_if, **where):
        sends.append((send_if, pltpu.make_async_remote_copy(
            src_ref=src, dst_ref=dst, send_sem=ssem.at[count[0]], recv_sem=rsem.at[slot],
            device_id=where, device_id_type=MESH)))
        count[0] += 1

    def plan_take(lvl, dst, slot, take_if):
        takes[lvl].append((take_if, pltpu.make_async_remote_copy(
            src_ref=dst, dst_ref=dst, send_sem=ssem.at[0], recv_sem=rsem.at[slot],
            device_id=dict(aper=(A + 1) % 32), device_id_type=MESH)))

    for e in range(2):
        plan_send(PS.at[0, e], PB0.at[c0], 22 + c0, c0 != e, aper=4 * (2 * (top // 2) + e) + low)
        plan_take(0, PB0.at[e], 22 + e, c0 != e)
        for side in range(2):
            plan_send(PS.at[0, e, 1 - side], PB0H.at[side, c0], 32 + 2 * side + c0, y_ok[1 - side],
                      aper=4 * (2 * (top // 2) + e) + low, ang=Y + 1 - 2 * side)
            plan_take(0, PB0H.at[side, e], 32 + 2 * side + e, y_ok[side])
    for q in range(4):
        plan_send(PS.at[1, q // 2], PB1.at[t10], 18 + t10, t10 != q, aper=4 * (t2 * 4 + q) + low)
        plan_take(1, PB1.at[q], 18 + q, t10 != q)
        for side in range(2):
            plan_send(PS.at[1, q // 2, 1 - side], PB1H.at[side, t10], 24 + 4 * side + t10, y_ok[1 - side],
                      aper=4 * (t2 * 4 + q) + low, ang=Y + 1 - 2 * side)
            plan_take(1, PB1H.at[side, q], 24 + 4 * side + q, y_ok[side])
    for t in range(8):
        plan_send(PS.at[2, t // 4], PB2.at[top], 10 + top, top != t, aper=4 * t + low)
        plan_take(2, PB2.at[t], 10 + t, top != t)

    pl.semaphore_wait(barrier, 31 + 4 * ny + nx + nx * ny)
    for send_if, _, copy in copies:
        pl.when(send_if)(copy.start)
    for send_if, copy in sends:
        pl.when(send_if)(copy.start)

    for _, take_if, copy in copies:
        pl.when(take_if)(copy.wait_recv)

    lane1 = lane_of((1, 128))
    k_q = jnp.where(k_at < 64, 256 + k_at, jnp.where(k_at < 192, k_at - 128, k_at))

    def packed(lo, hi, width):
        half = width // 2
        lane = lane_of(lo.shape)
        got = jnp.where(lane < half, pltpu.roll(lo, half, 1), pltpu.roll(hi, half, 1))
        got = jnp.where(lane < width, got, 0.0)
        step = width
        while step < 128:
            got = got + pltpu.roll(got, step, 1)
            step *= 2
        return got

    def beyond_tables(lvl):
        width = 16 >> lvl
        half = width // 2
        r0 = 16 * lvl
        tab = packed(TABH[0, r0:r0 + 16, :], TABH[1, r0:r0 + 16, :], width)

        def pick(first, second):
            return jnp.where(lane1 < 64, tab[first:first + 1], tab[second:second + 1])

        within = lane1 % width
        beam = jnp.where(within < half, within - half, 256 + within - half)
        lag = (k_q - beam).astype(F32) - pick(0, 1)
        full = tap_matrix(lag, [pick(8 + t, 12 + t) for t in range(4)])
        source = (lane1 // width) % (4 << lvl)
        dest = RHSH0 if lvl == 0 else RHSH1
        for m in range(4 << lvl):
            dest[m] = jnp.where(source == m, full, 0.0).astype(BF16)
        for k, row in enumerate(shift_rows(pick(2, 3), pick(4, 5))):
            WTH[lvl, k:k + 1, :] = row
        known = jnp.where(within < half, one(y_ok[0]), one(y_ok[1])) > 0

        def swing_halo(i, carry, lvl=lvl, rate=tab[6:7], known=known):
            first = pl.multiple_of(i * 16, 16)
            ramp, inside = ramp_of(first, lvl)
            cs = cos_sin(ramp * rate)
            ok = jnp.logical_and(inside, known)
            for k in range(2):
                EH[lvl, k, pl.ds(first, 16), :] = jnp.where(ok, cs[k], 0.0)
            return carry

        lax.fori_loop(0, 9, swing_halo, 0)

    def beyond_phases(lvl):
        width = 16 >> lvl
        owner = lane1 // width
        total = jnp.zeros((1, 128), F32)
        for q in range(2 << lvl):
            lo, hi = (PB0H[0, q], PB0H[1, q]) if lvl == 0 else (PB1H[0, q], PB1H[1, q])
            rows = packed(lo, hi, width)
            mine = 4 * q + row_of((4, 128)) == owner
            total = total + jnp.sum(jnp.where(mine, rows, 0.0), axis=0, keepdims=True)
        cs = cos_sin(total)
        for k in range(2):
            PCH[lvl, k, 0:1, :] = cs[k]

    left_half = lane_of((16, 128)) < 64

    def lay(dest, row, main0, main1, halo, beyond, main_too=True):
        rows = pl.ds(row, 16)
        if main_too:
            dest[0, rows, 0:128] = main0
            dest[1, rows, 0:128] = main1
        dest[0, rows, 128:256] = jnp.where(left_half, main1, halo)
        dest[1, rows, 128:256] = jnp.where(left_half, halo, main0)
        if beyond:
            dest[2, rows, 0:128] = halo
            dest[2, rows, 128:256] = jnp.where(left_half, main0, main1)

    for j in range(4):
        for ri in range(2):
            img = 2 * j + ri
            for first in range(0, 160, 16):
                lo = pltpu.roll(PH[0, first:first + 16, :].astype(F32), (128 - 16 * img - 16) % 128, 1)
                hi = pltpu.roll(PH[1, first:first + 16, :].astype(F32), (128 - 16 * img) % 128, 1)
                halo = jnp.where(left_half, hi, lo).astype(BF16)
                row = 320 * j + 160 * ri + first
                edge = first in (0, 144)
                main = [XR[img, b, first // 144] if edge else L0[b, row:row + 16, 0:128] for b in range(2)]
                lay(L0, row, main[0], main[1], halo, True, edge)

    def settle(src, at, dst, to, b4, b2, lvl, rows):
        d = ROWS_BELOW_IN[lvl] - ROWS_BELOW_OUT[lvl]
        for first in range(0, rows, 8):
            a, b, c, e = (src[at + (pl.ds(first + d + o, 8), slice(None))] for o in (-4, -2, 0, 2))
            dst[to + (pl.ds(first, 8), slice(None))] = jnp.where(b2, jnp.where(b4, e, b), jnp.where(b4, c, a))

    def three(src, at, first, w):
        return (
            w[0] * src[at + (pl.ds(first, 16), slice(None))]
            + w[1] * src[at + (pl.ds(first + 1, 16), slice(None))]
            + w[2] * src[at + (pl.ds(first + 2, 16), slice(None))]
        )

    def turn(re, im, c, s):
        return re * c - im * s, re * s + im * c

    for lvl in range(2):
        src, dst, tail = (L0, L1, RHSH0) if lvl == 0 else (L1, L2, RHSH1)
        rows = ROWS_IN[lvl]
        images = 4 << lvl
        width = 16 >> lvl
        phases = PC0 if lvl == 0 else PC1

        beyond_tables(lvl)
        for take_if, copy in takes[lvl]:
            pl.when(take_if)(copy.wait_recv)
        beyond_phases(lvl)
        if lvl == 0:
            for h0 in range(2):
                for b in range(2):
                    cs = cos_sin(PB0[h0, b])
                    PC0[h0, b, 0], PC0[h0, b, 1] = cs
        else:
            for q in range(4):
                for b in range(2):
                    cs = cos_sin(PB1[q, b])
                    PC1[q, b, 0], PC1[q, b, 1] = cs
        got = dot(src[2, 0:2 * rows, :], tail[0])
        for m in range(1, images):
            got = got + dot(src[2, 2 * rows * m:2 * rows * m + 2 * rows, :], tail[m])
        for ri in range(2):
            IH[ri, 0:rows, :] = got[rows * ri:rows * ri + rows]
            settle(IH, (ri,), S2H, (ri,), WTH[lvl, 0:1, :] > 0.5, WTH[lvl, 1:2, :] > 0.5, lvl, 152)
        w = [WTH[lvl, k:k + 1, :] for k in (2, 3, 4)]
        for first in range(0, 144, 16):
            re, im = three(S2H, (0,), first, w), three(S2H, (1,), first, w)
            re, im = turn(re, im, EH[lvl, 0, first:first + 16, :], EH[lvl, 1, first:first + 16, :])
            re, im = turn(re, im, PCH[lvl, 0, 0:1, :], PCH[lvl, 1, 0:1, :])
            HB[0, first:first + 16, :] = re
            HB[1, first:first + 16, :] = im

        def two_images(i, carry, lvl=lvl, src=src, dst=dst, rows=rows, images=images, width=width, phases=phases):
            for u in range(2):
                at = pl.multiple_of((2 * i + u) * (2 * rows), 2 * rows)
                for b in range(2):
                    got = dot(src[b, pl.ds(at, 2 * rows), :], RHS[lvl, b])
                    for h in range(2):
                        for ri in range(2):
                            IB[u, b, h, ri, 0:rows, :] = got[rows * ri:rows * ri + rows, 128 * h:128 * h + 128]
            for u in range(2):
                m = 2 * i + u
                q = m // 4
                j = m % 4
                w, turned, back = [], [], []
                for h in range(2):
                    for b in range(2):
                        b4 = WT[lvl, h, b, 0:1, :] > 0.5
                        b2 = WT[lvl, h, b, 1:2, :] > 0.5
                        for ri in range(2):
                            settle(IB, (u, b, h, ri), S2, (u, h, b, ri), b4, b2, lvl, 152)
                    w.append([[WT[lvl, h, b, k:k + 1, :] for k in (2, 3, 4)] for b in range(2)])
                    who = h if lvl == 0 else 2 * h + q
                    turned.append([[phases[who, b, k, pl.ds(j, 1), :] for k in range(2)] for b in range(2)])
                    back.append(128 - (width * (images * h + m) + width // 2))
                for first in range(0, 144, 16):
                    swings = [[EM[lvl, b, k, first:first + 16, :] for k in range(2)] for b in range(2)]
                    for h in range(2):
                        main = []
                        for b in range(2):
                            re, im = three(S2, (u, h, b, 0), first, w[h][b]), three(S2, (u, h, b, 1), first, w[h][b])
                            re, im = turn(re, im, swings[b][0], swings[b][1])
                            main.append(turn(re, im, turned[h][b][0], turned[h][b][1]))
                        for ri in range(2):
                            halo = pltpu.roll(HB[ri, first:first + 16, :], back[h], 1).astype(BF16)
                            row = pl.multiple_of((images * h + m) * 288 + 144 * ri + first, 16)
                            lay(dst, row, main[0][ri].astype(BF16), main[1][ri].astype(BF16), halo, lvl == 0)
            return carry

        lax.fori_loop(0, images // 2, two_images, 0)

    for take_if, copy in takes[2]:
        pl.when(take_if)(copy.wait_recv)
    for t in range(8):
        group = fp[16 * t:16 * t + 16, :]
        mine = group[0:4]
        for k in range(1, 4):
            mine = jnp.where(low == k, group[4 * k:4 * k + 4], mine)
        for b in range(2):
            cs = cos_sin(PB2[t, b] + mine[:, 128 * b:128 * b + 128])
            PC2[t, b, 0], PC2[t, b, 1] = cs

    def rs_copy(k):
        return pltpu.make_async_remote_copy(
            src_ref=SB.at[k], dst_ref=RS.at[A], send_sem=rs_ssem.at[k], recv_sem=rs_rsem.at[A],
            device_id=dict(aper=k), device_id_type=MESH)

    for b in range(2):
        ACC[...] = jnp.zeros((2, 2, 144, 128), F32)

        def gather(i, carry, b=b):
            at = pl.multiple_of(i * 1152, 1152)
            got = dot(L2[b, pl.ds(at, 1152), :], RHS[2, b])
            for h in range(2):
                c = [PC2[4 * h + i, b, 0, j:j + 1, :] for j in range(4)]
                s = [PC2[4 * h + i, b, 1, j:j + 1, :] for j in range(4)]
                for first in range(0, 136, 8):
                    re, im = ACC[h, 0, first:first + 8, :], ACC[h, 1, first:first + 8, :]
                    for j in range(4):
                        row = 288 * j + first
                        x = got[row:row + 8, 128 * h:128 * h + 128]
                        y = got[row + 144:row + 152, 128 * h:128 * h + 128]
                        re = re + (x * c[j] - y * s[j])
                        im = im + (x * s[j] + y * c[j])
                    ACC[h, 0, first:first + 8, :] = re
                    ACC[h, 1, first:first + 8, :] = im
            return carry

        lax.fori_loop(0, 4, gather, 0)
        for h in range(2):
            b4 = WT[2, h, b, 0:1, :] > 0.5
            b2 = WT[2, h, b, 1:2, :] > 0.5
            for ri in range(2):
                settle(ACC, (h, ri), S2, (0, h, b, ri), b4, b2, 2, 136)
        w = [[WT[2, h, b, k:k + 1, :] for k in (2, 3, 4)] for h in range(2)]
        for first in range(0, 128, 16):
            re = three(S2, (0, 0, b, 0), first, w[0]) + three(S2, (0, 1, b, 0), first, w[1])
            im = three(S2, (0, 0, b, 1), first, w[0]) + three(S2, (0, 1, b, 1), first, w[1])
            re, im = turn(re, im, EM[2, b, 0, first:first + 16, :], EM[2, b, 1, first:first + 16, :])
            FB[0, first:first + 16, :] = re.astype(BF16)
            FB[1, first:first + 16, :] = im.astype(BF16)
        parts = [lax.dot_general(eye, FB[ri], NT, preferred_element_type=F32).reshape(16, 8, 128) for ri in range(2)]
        SB[16 * b:16 * b + 16] = jnp.concatenate(parts, axis=1).astype(BF16)

        def send(k, carry):
            @pl.when(k != A)
            def _():
                rs_copy(k).start()
            return carry

        lax.fori_loop(16 * b, 16 * b + 16, send, 0)

    RS[A] = SB[A]

    def arrive(k, total):
        @pl.when(k != A)
        def _():
            pltpu.make_async_remote_copy(
                src_ref=SB.at[k], dst_ref=RS.at[k], send_sem=rs_ssem.at[k], recv_sem=rs_rsem.at[k],
                device_id=dict(aper=k), device_id_type=MESH).wait_recv()
        return total + RS[k].astype(F32)

    total = lax.fori_loop(0, 32, arrive, jnp.zeros((16, 128), F32)) * (1.0 / math.sqrt(128.0))
    out[0, 0] = total[0:8]
    out[1, 0] = total[8:16]

    for send_if, _, copy in copies:
        pl.when(send_if)(copy.wait_send)
    for send_if, copy in sends:
        pl.when(send_if)(copy.wait_send)

    def sent(k, carry):
        @pl.when(k != A)
        def _():
            rs_copy(k).wait_send()
        return carry

    lax.fori_loop(0, 32, sent, 0)


def body(*args):
    v = pltpu.VMEM
    return pl.pallas_call(
        kernel,
        out_shape=jax.ShapeDtypeStruct((2, 1, 8, 128), F32),
        in_specs=[pl.BlockSpec(memory_space=pltpu.HBM)] * 8,
        out_specs=pl.BlockSpec(memory_space=pltpu.VMEM),
        scratch_shapes=[v(a.shape, a.dtype) for a in args]
        + [
            pltpu.SemaphoreType.DMA((8,)),
            v((8, 2, 2, 16, 128), BF16),
            v((8, 2, 2, 16, 128), BF16),
            v((2, 128, 128), BF16),
            v((2, 160, 128), BF16),
            v((2, 48, 128), F32),
            v((2, 32, 128), F32),
            v((3, 2, 2, 4, 128), F32),
            v((8, 2, 4, 128), F32),
            v((4, 2, 4, 128), F32),
            v((2, 2, 4, 128), F32),
            v((2, 4, 4, 128), F32),
            v((2, 2, 4, 128), F32),
            v((3, 2, 256, 256), BF16),
            v((4, 256, 128), BF16),
            v((8, 256, 128), BF16),
            v((3, 2, 2, 8, 128), F32),
            v((2, 8, 128), F32),
            v((3, 2, 2, 144, 128), F32),
            v((2, 2, 144, 128), F32),
            v((8, 2, 2, 4, 128), F32),
            v((4, 2, 2, 4, 128), F32),
            v((2, 2, 2, 4, 128), F32),
            v((2, 2, 8, 128), F32),
            v((3, 4 * 320, 256), BF16),
            v((3, 8 * 288, 256), BF16),
            v((2, 16 * 288, 256), BF16),
            v((2, 2, 2, 2, 176, 128), F32),
            v((2, 176, 128), F32),
            v((2, 2, 2, 2, 160, 128), F32),
            v((2, 160, 128), F32),
            v((2, 144, 128), F32),
            v((2, 2, 144, 128), F32),
            v((2, 128, 128), BF16),
            v((32, 16, 128), BF16),
            v((32, 16, 128), BF16),
            pltpu.SemaphoreType.DMA((48,)),
            pltpu.SemaphoreType.DMA((48,)),
            pltpu.SemaphoreType.DMA((32,)),
            pltpu.SemaphoreType.DMA((32,)),
        ],
        compiler_params=pltpu.CompilerParams(collective_id=0, has_side_effects=True, vmem_limit_bytes=63 * 1024 * 1024),
    )(*args)


def solution(mesh):
    in_specs = (
        P("aper", None, "ang", "rng"),
        P(None, None, None, "ang"),
        P(None, None, None, "ang"),
        P(None, None, None, None, "ang"),
        P(None, None, None, "ang"),
        P("aper", None, None, "ang"),
        P(None, None, "ang"),
        P(None, "ang"),
    )
    out_specs = P(None, "ang", "aper", "rng")
    return jax.shard_map(body, mesh=mesh, in_specs=in_specs, out_specs=out_specs, check_vma=False)
```

```python
import functools
import math

import jax
import jax.numpy as jnp
from jax import lax
from jax.experimental import pallas as pl
from jax.experimental.pallas import tpu as pltpu
from jax.sharding import PartitionSpec as P

MESH = pl.DeviceIdType.MESH
F32 = jnp.float32
BF16 = jnp.bfloat16
I32 = jnp.int32

ROWS_BELOW_IN = (16, 8, 4)
ROWS_BELOW_OUT = (8, 4, 0)
ROWS_IN = (160, 144, 144)
ROWS_OUT = (144, 144, 128)
NT = (((1,), (1,)), ((), ()))

SIN_C = (0.9999999957158404, -0.16666657969904627, 0.008333050617327633, -0.0001980904635743576, 2.605166275944652e-06)
COS_C = (0.9999999997799074, -0.49999999356956554, 0.04166663620892635, -0.0013888360842520568, 2.4760135515714637e-05, -2.605107635999247e-07)


def cos_sin(angle):
    turns = jnp.floor(angle * (0.5 / math.pi) + 0.5)
    rest = (angle - turns * 6.28125) - turns * (2 * math.pi - 6.28125)
    half = 0.5 * rest
    sq = half * half
    s = jnp.full_like(sq, SIN_C[-1])
    for coef in SIN_C[-2::-1]:
        s = s * sq + coef
    s = s * half
    c = jnp.full_like(sq, COS_C[-1])
    for coef in COS_C[-2::-1]:
        c = c * sq + coef
    return 1.0 - 2.0 * s * s, 2.0 * s * c


def lane_of(shape):
    return lax.broadcasted_iota(I32, shape, len(shape) - 1)


def row_of(shape):
    return lax.broadcasted_iota(I32, shape, len(shape) - 2)


def dot(a, b):
    return jnp.dot(a, b, preferred_element_type=F32)


def shift_rows(range_offset, fraction):
    o = range_offset + 4.0
    b4 = jnp.where(o >= 4.0, 1.0, 0.0)
    o = o - 4.0 * b4
    b2 = jnp.where(o >= 2.0, 1.0, 0.0)
    b1 = o - 2.0 * b2
    return b4, b2, (1.0 - b1) * (1.0 - fraction), (1.0 - b1) * fraction + b1 * (1.0 - fraction), b1 * fraction


def tap_matrix(lag, taps):
    out = jnp.where(lag == 3.0, taps[3], 0.0)
    for t in (2, 1, 0):
        out = jnp.where(lag == float(t), taps[t], out)
    return out


def kernel(
    *refs,
):
    ins, rest = refs[:8], refs[8:]
    out = rest[0]
    here = rest[1:9]
    in_sem = rest[9]
    (sub, bo, ro, bt, rf, pb, pr, fp) = here
    (
    XS, XR, PE, PH, TAB, TABH, PS, PB2, PB1, PB0, PB1H, PB0H,
    RHS, RHSH0, RHSH1, WT, WTH, EM, EH, PC2, PC1, PC0, PCH,
    L0, L1, L2, IB, IH, S2, S2H, HB, ACC, FB, SB, RS,
    ssem, rsem, rs_ssem, rs_rsem,
    ) = rest[10:]
    loads = [pltpu.make_async_copy(ins[k], here[k], in_sem.at[k]) for k in (5, 0, 1, 2, 3, 4, 6, 7)]
    for load in loads:
        load.start()
    A = lax.axis_index("aper")
    X = lax.axis_index("rng")
    Y = lax.axis_index("ang")
    top = A // 4
    low = A % 4
    c2 = top // 4
    c1 = (top // 2) % 2
    c0 = top % 2
    cbits = (c0, c1, c2)
    t2 = c2
    t10 = top % 4

    barrier = pltpu.get_barrier_semaphore()

    def tell(**where):
        pl.semaphore_signal(barrier, inc=1, device_id=where, device_id_type=MESH)

    def tell_aper(k, carry):
        tell(aper=(A + k) % 32)
        return carry

    lax.fori_loop(1, 32, tell_aper, 0)
    y_ok = (Y > 0, Y < 3)
    x_ok = (X > 0, X < 3)
    for dy, ok_y in ((-1, y_ok[0]), (1, y_ok[1])):
        @pl.when(ok_y)
        def _():
            for q in range(4):
                tell(aper=4 * (t2 * 4 + q) + low, ang=Y + dy)
    for dx, ok_x in ((-1, x_ok[0]), (1, x_ok[1])):
        @pl.when(ok_x)
        def _():
            tell(rng=X + dx)
        for dy, ok_y in ((-1, y_ok[0]), (1, y_ok[1])):
            @pl.when(jnp.logical_and(ok_x, ok_y))
            def _():
                tell(rng=X + dx, ang=Y + dy)
    one = lambda ok: jnp.where(ok, 1, 0).astype(I32)
    ny = one(y_ok[0]) + one(y_ok[1])
    nx = one(x_ok[0]) + one(x_ok[1])

    for load in loads:
        load.wait()

    eye = jnp.where(row_of((128, 128)) == lane_of((128, 128)), 1.0, 0.0).astype(BF16)
    for j in range(4):
        for ri in range(2):
            turned = lax.dot_general(eye, sub[j, ri], NT, preferred_element_type=F32).astype(BF16)
            for b in range(2):
                main = turned[:, 128 * b:128 * b + 128]
                L0[b, 320 * j + 160 * ri + 16:320 * j + 160 * ri + 144, 0:128] = main
                XS[0, 2 * j + ri, b] = main[0:16]
                XS[1, 2 * j + ri, b] = main[112:128]
    for side, first in ((0, 0), (1, 240)):
        edge = sub[:, :, first:first + 16, :].reshape(128, 128)
        PE[side] = lax.dot_general(eye, edge, NT, preferred_element_type=F32).astype(BF16)

    for lvl in range(3):
        c = cbits[lvl]
        offs = bo[lvl, c].astype(F32)
        rofs = ro[lvl, c].astype(F32)
        frac = rf[lvl, c]
        taps = bt[lvl, c].astype(F32)
        rates = pr[lvl]
        rate = jnp.where(c == 0, rates[0:1], rates[1:2])
        for b in range(2):
            cut = slice(128 * b, 128 * b + 128)
            r0 = 16 * lvl
            TAB[b, r0:r0 + 2, :] = offs[:, cut]
            TAB[b, r0 + 2:r0 + 4, :] = rofs[:, cut]
            TAB[b, r0 + 4:r0 + 6, :] = frac[:, cut]
            TAB[b, r0 + 6:r0 + 7, :] = rate[:, cut]
            TAB[b, r0 + 7:r0 + 8, :] = rate[:, cut]
            TAB[b, r0 + 8:r0 + 12, :] = taps[0, :, cut]
            TAB[b, r0 + 12:r0 + 16, :] = taps[1, :, cut]
    for j in range(4):
        for lvl in range(3):
            base = pb[j, lvl]
            for c in range(2):
                for b in range(2):
                    PS[lvl, c, b, j:j + 1, :] = base[c:c + 1, 128 * b:128 * b + 128]
    PB2[top] = PS[2, c2]
    PB1[t10] = PS[1, c1]
    PB0[c0] = PS[0, c0]
    SHARED = 32

    @pl.when(X == 0)
    def _():
        XR[0] = jnp.zeros((8, 2, 16, 128), BF16)
        PH[:, 0:16, :] = jnp.zeros((2, 16, 128), BF16)

    @pl.when(X == 3)
    def _():
        XR[1] = jnp.zeros((8, 2, 16, 128), BF16)
        PH[:, 144:160, :] = jnp.zeros((2, 16, 128), BF16)

    for side, edge_at in ((0, 0), (1, 3)):
        @pl.when(Y == edge_at)
        def _():
            PH[side] = jnp.zeros((160, 128), BF16)
            TABH[side] = jnp.zeros((SHARED, 128), F32)
            PB1H[side] = jnp.zeros((4, 4, 128), F32)
            PB0H[side] = jnp.zeros((2, 4, 128), F32)

    copies = []
    count = [0]

    def plan(src, dst, slot, send_if, take_if, **where):
        copies.append((
            send_if, take_if,
            pltpu.make_async_remote_copy(
                src_ref=src, dst_ref=dst, send_sem=ssem.at[count[0]], recv_sem=rsem.at[slot],
                device_id=where, device_id_type=MESH,
            ),
        ))
        count[0] += 1

    plan(XS.at[1], XR.at[0], 0, x_ok[1], x_ok[0], rng=X + 1)
    plan(XS.at[0], XR.at[1], 1, x_ok[0], x_ok[1], rng=X - 1)
    both = jnp.logical_and
    for side in range(2):
        dy = 1 - 2 * side
        send_y, take_y = y_ok[1 - side], y_ok[side]
        edge = PE.at[1 - side]
        plan(edge, PH.at[side, pl.ds(16, 128), :], 2 + side, send_y, take_y, ang=Y + dy)
        plan(edge.at[pl.ds(112, 16), :], PH.at[side, pl.ds(0, 16), :], 4 + side,
             both(send_y, x_ok[1]), both(take_y, x_ok[0]), rng=X + 1, ang=Y + dy)
        plan(edge.at[pl.ds(0, 16), :], PH.at[side, pl.ds(144, 16), :], 6 + side,
             both(send_y, x_ok[0]), both(take_y, x_ok[1]), rng=X - 1, ang=Y + dy)
        plan(TAB.at[1 - side, pl.ds(0, SHARED), :], TABH.at[side], 8 + side, send_y, take_y, ang=Y + dy)
    sends = []
    takes = ([], [], [])

    def plan_send(src, dst, slot, send_if, **where):
        sends.append((send_if, pltpu.make_async_remote_copy(
            src_ref=src, dst_ref=dst, send_sem=ssem.at[count[0]], recv_sem=rsem.at[slot],
            device_id=where, device_id_type=MESH)))
        count[0] += 1

    def plan_take(lvl, dst, slot, take_if):
        takes[lvl].append((take_if, pltpu.make_async_remote_copy(
            src_ref=dst, dst_ref=dst, send_sem=ssem.at[0], recv_sem=rsem.at[slot],
            device_id=dict(aper=(A + 1) % 32), device_id_type=MESH)))

    for e in range(2):
        plan_send(PS.at[0, e], PB0.at[c0], 22 + c0, c0 != e, aper=4 * (2 * (top // 2) + e) + low)
        plan_take(0, PB0.at[e], 22 + e, c0 != e)
        for side in range(2):
            plan_send(PS.at[0, e, 1 - side], PB0H.at[side, c0], 32 + 2 * side + c0, y_ok[1 - side],
                      aper=4 * (2 * (top // 2) + e) + low, ang=Y + 1 - 2 * side)
            plan_take(0, PB0H.at[side, e], 32 + 2 * side + e, y_ok[side])
    for q in range(4):
        plan_send(PS.at[1, q // 2], PB1.at[t10], 18 + t10, t10 != q, aper=4 * (t2 * 4 + q) + low)
        plan_take(1, PB1.at[q], 18 + q, t10 != q)
        for side in range(2):
            plan_send(PS.at[1, q // 2, 1 - side], PB1H.at[side, t10], 24 + 4 * side + t10, y_ok[1 - side],
                      aper=4 * (t2 * 4 + q) + low, ang=Y + 1 - 2 * side)
            plan_take(1, PB1H.at[side, q], 24 + 4 * side + q, y_ok[side])
    for t in range(8):
        plan_send(PS.at[2, t // 4], PB2.at[top], 10 + top, top != t, aper=4 * t + low)
        plan_take(2, PB2.at[t], 10 + t, top != t)

    pl.semaphore_wait(barrier, 31 + 4 * ny + nx + nx * ny)
    for send_if, _, copy in copies:
        pl.when(send_if)(copy.start)
    for send_if, copy in sends:
        pl.when(send_if)(copy.start)

    k_at = row_of((256, 128))
    near = (jnp.where(k_at < 192, k_at, k_at - 256) - lane_of((256, 128))).astype(F32)
    for lvl in range(3):
        r0 = 16 * lvl
        for b in range(2):
            for h in range(2):
                lag = near - TAB[b, r0 + h:r0 + h + 1, :]
                taps = [TAB[b, r0 + 8 + 4 * h + t:r0 + 9 + 4 * h + t, :] for t in range(4)]
                RHS[lvl, b, :, 128 * h:128 * h + 128] = tap_matrix(lag, taps).astype(BF16)
                rows = shift_rows(TAB[b, r0 + 2 + h:r0 + 3 + h, :], TAB[b, r0 + 4 + h:r0 + 5 + h, :])
                for k, row in enumerate(rows):
                    WT[lvl, h, b, k:k + 1, :] = row

    def ramp_of(first, lvl):
        at = X * 128 - ROWS_BELOW_OUT[lvl] + first + row_of((16, 128))
        inside = jnp.logical_and(at >= 0, at < 512)
        return at.astype(F32) * (1.0 / 512) - 0.5, inside

    def swing(i, carry):
        first = pl.multiple_of(i * 16, 16)
        for lvl in range(3):
            ramp, inside = ramp_of(first, lvl)
            for b in range(2):
                cs = cos_sin(ramp * TAB[b, 16 * lvl + 6:16 * lvl + 7, :])
                for k in range(2):
                    EM[lvl, b, k, pl.ds(first, 16), :] = jnp.where(inside, cs[k], 0.0)
        return carry

    lax.fori_loop(0, 9, swing, 0)

    for _, take_if, copy in copies:
        pl.when(take_if)(copy.wait_recv)

    lane1 = lane_of((1, 128))
    k_q = jnp.where(k_at < 64, 256 + k_at, jnp.where(k_at < 192, k_at - 128, k_at))

    def packed(lo, hi, width):
        half = width // 2
        lane = lane_of(lo.shape)
        got = jnp.where(lane < half, pltpu.roll(lo, half, 1), pltpu.roll(hi, half, 1))
        got = jnp.where(lane < width, got, 0.0)
        step = width
        while step < 128:
            got = got + pltpu.roll(got, step, 1)
            step *= 2
        return got

    def beyond_tables(lvl):
        width = 16 >> lvl
        half = width // 2
        r0 = 16 * lvl
        tab = packed(TABH[0, r0:r0 + 16, :], TABH[1, r0:r0 + 16, :], width)

        def pick(first, second):
            return jnp.where(lane1 < 64, tab[first:first + 1], tab[second:second + 1])

        within = lane1 % width
        beam = jnp.where(within < half, within - half, 256 + within - half)
        lag = (k_q - beam).astype(F32) - pick(0, 1)
        full = tap_matrix(lag, [pick(8 + t, 12 + t) for t in range(4)])
        source = (lane1 // width) % (4 << lvl)
        dest = RHSH0 if lvl == 0 else RHSH1
        for m in range(4 << lvl):
            dest[m] = jnp.where(source == m, full, 0.0).astype(BF16)
        for k, row in enumerate(shift_rows(pick(2, 3), pick(4, 5))):
            WTH[lvl, k:k + 1, :] = row
        known = jnp.where(within < half, one(y_ok[0]), one(y_ok[1])) > 0

        def swing_halo(i, carry, lvl=lvl, rate=tab[6:7], known=known):
            first = pl.multiple_of(i * 16, 16)
            ramp, inside = ramp_of(first, lvl)
            cs = cos_sin(ramp * rate)
            ok = jnp.logical_and(inside, known)
            for k in range(2):
                EH[lvl, k, pl.ds(first, 16), :] = jnp.where(ok, cs[k], 0.0)
            return carry

        lax.fori_loop(0, 9, swing_halo, 0)

    def beyond_phases(lvl):
        width = 16 >> lvl
        owner = lane1 // width
        total = jnp.zeros((1, 128), F32)
        for q in range(2 << lvl):
            lo, hi = (PB0H[0, q], PB0H[1, q]) if lvl == 0 else (PB1H[0, q], PB1H[1, q])
            rows = packed(lo, hi, width)
            mine = 4 * q + row_of((4, 128)) == owner
            total = total + jnp.sum(jnp.where(mine, rows, 0.0), axis=0, keepdims=True)
        cs = cos_sin(total)
        for k in range(2):
            PCH[lvl, k, 0:1, :] = cs[k]

    left_half = lane_of((16, 128)) < 64

    def lay(dest, row, main0, main1, halo, beyond, main_too=True):
        rows = pl.ds(row, 16)
        if main_too:
            dest[0, rows, 0:128] = main0
            dest[1, rows, 0:128] = main1
        dest[0, rows, 128:256] = jnp.where(left_half, main1, halo)
        dest[1, rows, 128:256] = jnp.where(left_half, halo, main0)
        if beyond:
            dest[2, rows, 0:128] = halo
            dest[2, rows, 128:256] = jnp.where(left_half, main0, main1)

    for j in range(4):
        for ri in range(2):
            img = 2 * j + ri
            for first in range(0, 160, 16):
                lo = pltpu.roll(PH[0, first:first + 16, :].astype(F32), (128 - 16 * img - 16) % 128, 1)
                hi = pltpu.roll(PH[1, first:first + 16, :].astype(F32), (128 - 16 * img) % 128, 1)
                halo = jnp.where(left_half, hi, lo).astype(BF16)
                row = 320 * j + 160 * ri + first
                edge = first in (0, 144)
                main = [XR[first // 144, img, b] if edge else L0[b, row:row + 16, 0:128] for b in range(2)]
                lay(L0, row, main[0], main[1], halo, True, edge)

    def settle(src, at, dst, to, b4, b2, lvl, rows):
        d = ROWS_BELOW_IN[lvl] - ROWS_BELOW_OUT[lvl]
        for first in range(0, rows, 8):
            a, b, c, e = (src[at + (pl.ds(first + d + o, 8), slice(None))] for o in (-4, -2, 0, 2))
            dst[to + (pl.ds(first, 8), slice(None))] = jnp.where(b2, jnp.where(b4, e, b), jnp.where(b4, c, a))

    def three(src, at, first, w):
        return (
            w[0] * src[at + (pl.ds(first, 16), slice(None))]
            + w[1] * src[at + (pl.ds(first + 1, 16), slice(None))]
            + w[2] * src[at + (pl.ds(first + 2, 16), slice(None))]
        )

    def turn(re, im, c, s):
        return re * c - im * s, re * s + im * c

    for lvl in range(2):
        src, dst, tail = (L0, L1, RHSH0) if lvl == 0 else (L1, L2, RHSH1)
        rows = ROWS_IN[lvl]
        images = 4 << lvl
        width = 16 >> lvl
        phases = PC0 if lvl == 0 else PC1

        beyond_tables(lvl)
        for take_if, copy in takes[lvl]:
            pl.when(take_if)(copy.wait_recv)
        beyond_phases(lvl)
        if lvl == 0:
            for h0 in range(2):
                for b in range(2):
                    cs = cos_sin(PB0[h0, b])
                    PC0[h0, b, 0], PC0[h0, b, 1] = cs
        else:
            for q in range(4):
                for b in range(2):
                    cs = cos_sin(PB1[q, b])
                    PC1[q, b, 0], PC1[q, b, 1] = cs
        got = dot(src[2, 0:2 * rows, :], tail[0])
        for m in range(1, images):
            got = got + dot(src[2, 2 * rows * m:2 * rows * m + 2 * rows, :], tail[m])
        for ri in range(2):
            IH[ri, 0:rows, :] = got[rows * ri:rows * ri + rows]
            settle(IH, (ri,), S2H, (ri,), WTH[lvl, 0:1, :] > 0.5, WTH[lvl, 1:2, :] > 0.5, lvl, 152)
        w = [WTH[lvl, k:k + 1, :] for k in (2, 3, 4)]
        for first in range(0, 144, 16):
            re, im = three(S2H, (0,), first, w), three(S2H, (1,), first, w)
            re, im = turn(re, im, EH[lvl, 0, first:first + 16, :], EH[lvl, 1, first:first + 16, :])
            re, im = turn(re, im, PCH[lvl, 0, 0:1, :], PCH[lvl, 1, 0:1, :])
            HB[0, first:first + 16, :] = re
            HB[1, first:first + 16, :] = im

        def two_images(i, carry, lvl=lvl, src=src, dst=dst, rows=rows, images=images, width=width, phases=phases):
            for u in range(2):
                at = pl.multiple_of((2 * i + u) * (2 * rows), 2 * rows)
                for b in range(2):
                    got = dot(src[b, pl.ds(at, 2 * rows), :], RHS[lvl, b])
                    for h in range(2):
                        for ri in range(2):
                            IB[u, b, h, ri, 0:rows, :] = got[rows * ri:rows * ri + rows, 128 * h:128 * h + 128]
            for u in range(2):
                m = 2 * i + u
                q = m // 4
                j = m % 4
                w, turned, back = [], [], []
                for h in range(2):
                    for b in range(2):
                        b4 = WT[lvl, h, b, 0:1, :] > 0.5
                        b2 = WT[lvl, h, b, 1:2, :] > 0.5
                        for ri in range(2):
                            settle(IB, (u, b, h, ri), S2, (u, h, b, ri), b4, b2, lvl, 152)
                    w.append([[WT[lvl, h, b, k:k + 1, :] for k in (2, 3, 4)] for b in range(2)])
                    who = h if lvl == 0 else 2 * h + q
                    turned.append([[phases[who, b, k, pl.ds(j, 1), :] for k in range(2)] for b in range(2)])
                    back.append(128 - (width * (images * h + m) + width // 2))
                for first in range(0, 144, 16):
                    swings = [[EM[lvl, b, k, first:first + 16, :] for k in range(2)] for b in range(2)]
                    for h in range(2):
                        main = []
                        for b in range(2):
                            re, im = three(S2, (u, h, b, 0), first, w[h][b]), three(S2, (u, h, b, 1), first, w[h][b])
                            re, im = turn(re, im, swings[b][0], swings[b][1])
                            main.append(turn(re, im, turned[h][b][0], turned[h][b][1]))
                        for ri in range(2):
                            halo = pltpu.roll(HB[ri, first:first + 16, :], back[h], 1).astype(BF16)
                            row = pl.multiple_of((images * h + m) * 288 + 144 * ri + first, 16)
                            lay(dst, row, main[0][ri].astype(BF16), main[1][ri].astype(BF16), halo, lvl == 0)
            return carry

        lax.fori_loop(0, images // 2, two_images, 0)

    for take_if, copy in takes[2]:
        pl.when(take_if)(copy.wait_recv)
    for t in range(8):
        group = fp[16 * t:16 * t + 16, :]
        mine = group[0:4]
        for k in range(1, 4):
            mine = jnp.where(low == k, group[4 * k:4 * k + 4], mine)
        for b in range(2):
            cs = cos_sin(PB2[t, b] + mine[:, 128 * b:128 * b + 128])
            PC2[t, b, 0], PC2[t, b, 1] = cs

    def rs_copy(k):
        return pltpu.make_async_remote_copy(
            src_ref=SB.at[k], dst_ref=RS.at[A], send_sem=rs_ssem, recv_sem=rs_rsem,
            device_id=dict(aper=k), device_id_type=MESH)

    own_half = A // 16
    for step in range(2):
        b = step
        for i in range(4):
            got = dot(L2[b, 1152 * i:1152 * i + 1152, :], RHS[2, b])
            for h in range(2):
                c = [PC2[4 * h + i, b, 0, j:j + 1, :] for j in range(4)]
                s = [PC2[4 * h + i, b, 1, j:j + 1, :] for j in range(4)]
                for first in range(0, 136, 8):
                    if i:
                        re, im = ACC[h, 0, first:first + 8, :], ACC[h, 1, first:first + 8, :]
                    for j in range(4):
                        row = 288 * j + first
                        x = got[row:row + 8, 128 * h:128 * h + 128]
                        y = got[row + 144:row + 152, 128 * h:128 * h + 128]
                        x, y = turn(x, y, c[j], s[j])
                        re, im = (re + x, im + y) if i or j else (x, y)
                    ACC[h, 0, first:first + 8, :] = re
                    ACC[h, 1, first:first + 8, :] = im
        for h in range(2):
            b4 = WT[2, h, b, 0:1, :] > 0.5
            b2 = WT[2, h, b, 1:2, :] > 0.5
            for ri in range(2):
                settle(ACC, (h, ri), S2, (step, h, 0, ri), b4, b2, 2, 136)
        w = [[WT[2, h, b, k:k + 1, :] for k in (2, 3, 4)] for h in range(2)]
        for first in range(0, 128, 16):
            re = three(S2, (step, 0, 0, 0), first, w[0]) + three(S2, (step, 1, 0, 0), first, w[1])
            im = three(S2, (step, 0, 0, 1), first, w[0]) + three(S2, (step, 1, 0, 1), first, w[1])
            re, im = turn(re, im, EM[2, b, 0, first:first + 16, :], EM[2, b, 1, first:first + 16, :])
            FB[0, first:first + 16, :] = re.astype(BF16)
            FB[1, first:first + 16, :] = im.astype(BF16)
        parts = [lax.dot_general(eye, FB[ri], NT, preferred_element_type=F32).reshape(16, 8, 128) for ri in range(2)]
        SB[pl.ds(16 * b, 16)] = jnp.concatenate(parts, axis=1).astype(BF16)

        def send(i, carry, b=b):
            k = 16 * b + i

            @pl.when(k != A)
            def _():
                rs_copy(k).start()
            return carry

        lax.fori_loop(0, 16, send, 0)

    RS[A] = SB[A]

    for send_if, _, copy in copies:
        pl.when(send_if)(copy.wait_send)
    for send_if, copy in sends:
        pl.when(send_if)(copy.wait_send)

    some = pl.ds(0, 31)
    everything = pltpu.make_async_remote_copy(
        src_ref=SB.at[some], dst_ref=RS.at[some], send_sem=rs_ssem, recv_sem=rs_rsem,
        device_id=dict(aper=(A + 1) % 32), device_id_type=MESH)
    everything.wait_recv()
    parts = [RS[k].astype(F32) for k in range(32)]
    while len(parts) > 1:
        parts = [parts[k] + parts[k + 1] for k in range(0, len(parts), 2)]
    total = parts[0] * (1.0 / math.sqrt(128.0))
    out[0, 0] = total[0:8]
    out[1, 0] = total[8:16]
    everything.wait_send()


def body(*args):
    v = pltpu.VMEM
    return pl.pallas_call(
        kernel,
        out_shape=jax.ShapeDtypeStruct((2, 1, 8, 128), F32),
        in_specs=[pl.BlockSpec(memory_space=pltpu.HBM)] * 8,
        out_specs=pl.BlockSpec(memory_space=pltpu.VMEM),
        scratch_shapes=[v(a.shape, a.dtype) for a in args]
        + [
            pltpu.SemaphoreType.DMA((8,)),
            v((2, 8, 2, 16, 128), BF16),
            v((2, 8, 2, 16, 128), BF16),
            v((2, 128, 128), BF16),
            v((2, 160, 128), BF16),
            v((2, 48, 128), F32),
            v((2, 32, 128), F32),
            v((3, 2, 2, 4, 128), F32),
            v((8, 2, 4, 128), F32),
            v((4, 2, 4, 128), F32),
            v((2, 2, 4, 128), F32),
            v((2, 4, 4, 128), F32),
            v((2, 2, 4, 128), F32),
            v((3, 2, 256, 256), BF16),
            v((4, 256, 128), BF16),
            v((8, 256, 128), BF16),
            v((3, 2, 2, 8, 128), F32),
            v((2, 8, 128), F32),
            v((3, 2, 2, 144, 128), F32),
            v((2, 2, 144, 128), F32),
            v((8, 2, 2, 4, 128), F32),
            v((4, 2, 2, 4, 128), F32),
            v((2, 2, 2, 4, 128), F32),
            v((2, 2, 8, 128), F32),
            v((3, 4 * 320, 256), BF16),
            v((3, 8 * 288, 256), BF16),
            v((2, 16 * 288, 256), BF16),
            v((2, 2, 2, 2, 176, 128), F32),
            v((2, 176, 128), F32),
            v((2, 2, 2, 2, 160, 128), F32),
            v((2, 160, 128), F32),
            v((2, 144, 128), F32),
            v((2, 2, 144, 128), F32),
            v((2, 128, 128), BF16),
            v((32, 16, 128), BF16),
            v((32, 16, 128), BF16),
            pltpu.SemaphoreType.DMA((48,)),
            pltpu.SemaphoreType.DMA((48,)),
            pltpu.SemaphoreType.DMA,
            pltpu.SemaphoreType.DMA,
        ],
        compiler_params=pltpu.CompilerParams(collective_id=0, has_side_effects=True, vmem_limit_bytes=63 * 1024 * 1024),
    )(*args)


def solution(mesh):
    in_specs = (
        P("aper", None, "ang", "rng"),
        P(None, None, None, "ang"),
        P(None, None, None, "ang"),
        P(None, None, None, None, "ang"),
        P(None, None, None, "ang"),
        P("aper", None, None, "ang"),
        P(None, None, "ang"),
        P(None, "ang"),
    )
    out_specs = P(None, "ang", "aper", "rng")
    return jax.shard_map(body, mesh=mesh, in_specs=in_specs, out_specs=out_specs, check_vma=False)
```

```python
import functools
import math

import jax
import jax.numpy as jnp
from jax import lax
from jax.experimental import pallas as pl
from jax.experimental.pallas import tpu as pltpu
from jax.sharding import PartitionSpec as P

MESH = pl.DeviceIdType.MESH
F32 = jnp.float32
BF16 = jnp.bfloat16
I32 = jnp.int32

ROWS_BELOW_IN = (16, 8, 4)
ROWS_BELOW_OUT = (8, 4, 0)
ROWS_IN = (160, 144, 144)
ROWS_OUT = (144, 144, 128)
NT = (((1,), (1,)), ((), ()))

SIN_C = (0.9999999957158404, -0.16666657969904627, 0.008333050617327633, -0.0001980904635743576, 2.605166275944652e-06)
COS_C = (0.9999999997799074, -0.49999999356956554, 0.04166663620892635, -0.0013888360842520568, 2.4760135515714637e-05, -2.605107635999247e-07)


def cos_sin(angle):
    turns = jnp.floor(angle * (0.5 / math.pi) + 0.5)
    rest = (angle - turns * 6.28125) - turns * (2 * math.pi - 6.28125)
    half = 0.5 * rest
    sq = half * half
    s = jnp.full_like(sq, SIN_C[-1])
    for coef in SIN_C[-2::-1]:
        s = s * sq + coef
    s = s * half
    c = jnp.full_like(sq, COS_C[-1])
    for coef in COS_C[-2::-1]:
        c = c * sq + coef
    return 1.0 - 2.0 * s * s, 2.0 * s * c


def lane_of(shape):
    return lax.broadcasted_iota(I32, shape, len(shape) - 1)


def row_of(shape):
    return lax.broadcasted_iota(I32, shape, len(shape) - 2)


def dot(a, b):
    return jnp.dot(a, b, preferred_element_type=F32)


def shift_rows(range_offset, fraction):
    o = range_offset + 4.0
    b4 = jnp.where(o >= 4.0, 1.0, 0.0)
    o = o - 4.0 * b4
    b2 = jnp.where(o >= 2.0, 1.0, 0.0)
    b1 = o - 2.0 * b2
    return b4, b2, (1.0 - b1) * (1.0 - fraction), (1.0 - b1) * fraction + b1 * (1.0 - fraction), b1 * fraction


def tap_matrix(lag, taps):
    out = jnp.where(lag == 3.0, taps[3], 0.0)
    for t in (2, 1, 0):
        out = jnp.where(lag == float(t), taps[t], out)
    return out


def kernel(
    *refs,
):
    ins, rest = refs[:8], refs[8:]
    out = rest[0]
    here = rest[1:9]
    in_sem = rest[9]
    (sub, bo, ro, bt, rf, pb, pr, fp) = here
    (
    XS, XR, PE, PH, TAB, TABH, PS, PB2, PB1, PB0, PB1H, PB0H,
    RHS, RHSH0, RHSH1, WT, WTH, EM, EH, PC2, PC1, PC0, PCH,
    L0, L1, L2, IB, IH, S2, S2H, HB, ACC, FB, SB, RS,
    ssem, rsem, rs_ssem, rs_rsem,
    ) = rest[10:]
    loads = [pltpu.make_async_copy(ins[k], here[k], in_sem.at[k]) for k in (5, 0, 1, 2, 3, 4, 6, 7)]
    for load in loads:
        load.start()
    A = lax.axis_index("aper")
    X = lax.axis_index("rng")
    Y = lax.axis_index("ang")
    top = A // 4
    low = A % 4
    c2 = top // 4
    c1 = (top // 2) % 2
    c0 = top % 2
    cbits = (c0, c1, c2)
    t2 = c2
    t10 = top % 4

    barrier = pltpu.get_barrier_semaphore()

    def tell(**where):
        pl.semaphore_signal(barrier, inc=1, device_id=where, device_id_type=MESH)

    def tell_aper(k, carry):
        tell(aper=(A + k) % 32)
        return carry

    lax.fori_loop(1, 32, tell_aper, 0)
    y_ok = (Y > 0, Y < 3)
    x_ok = (X > 0, X < 3)
    for dy, ok_y in ((-1, y_ok[0]), (1, y_ok[1])):
        @pl.when(ok_y)
        def _():
            for q in range(4):
                tell(aper=4 * (t2 * 4 + q) + low, ang=Y + dy)
    for dx, ok_x in ((-1, x_ok[0]), (1, x_ok[1])):
        @pl.when(ok_x)
        def _():
            tell(rng=X + dx)
        for dy, ok_y in ((-1, y_ok[0]), (1, y_ok[1])):
            @pl.when(jnp.logical_and(ok_x, ok_y))
            def _():
                tell(rng=X + dx, ang=Y + dy)
    one = lambda ok: jnp.where(ok, 1, 0).astype(I32)
    ny = one(y_ok[0]) + one(y_ok[1])
    nx = one(x_ok[0]) + one(x_ok[1])

    for load in loads:
        load.wait()

    eye = jnp.where(row_of((128, 128)) == lane_of((128, 128)), 1.0, 0.0).astype(BF16)
    for j in range(4):
        for ri in range(2):
            turned = lax.dot_general(eye, sub[j, ri], NT, preferred_element_type=F32).astype(BF16)
            for b in range(2):
                main = turned[:, 128 * b:128 * b + 128]
                L0[b, 320 * j + 160 * ri + 16:320 * j + 160 * ri + 144, 0:128] = main
                XS[0, 2 * j + ri, b] = main[0:16]
                XS[1, 2 * j + ri, b] = main[112:128]
    for side, first in ((0, 0), (1, 240)):
        edge = sub[:, :, first:first + 16, :].reshape(128, 128)
        PE[side] = lax.dot_general(eye, edge, NT, preferred_element_type=F32).astype(BF16)

    for lvl in range(3):
        c = cbits[lvl]
        offs = bo[lvl, c].astype(F32)
        rofs = ro[lvl, c].astype(F32)
        frac = rf[lvl, c]
        taps = bt[lvl, c].astype(F32)
        rates = pr[lvl]
        rate = jnp.where(c == 0, rates[0:1], rates[1:2])
        for b in range(2):
            cut = slice(128 * b, 128 * b + 128)
            r0 = 16 * lvl
            TAB[b, r0:r0 + 2, :] = offs[:, cut]
            TAB[b, r0 + 2:r0 + 4, :] = rofs[:, cut]
            TAB[b, r0 + 4:r0 + 6, :] = frac[:, cut]
            TAB[b, r0 + 6:r0 + 7, :] = rate[:, cut]
            TAB[b, r0 + 7:r0 + 8, :] = rate[:, cut]
            TAB[b, r0 + 8:r0 + 12, :] = taps[0, :, cut]
            TAB[b, r0 + 12:r0 + 16, :] = taps[1, :, cut]
    for j in range(4):
        for lvl in range(3):
            base = pb[j, lvl]
            for c in range(2):
                for b in range(2):
                    PS[lvl, c, b, j:j + 1, :] = base[c:c + 1, 128 * b:128 * b + 128]
    PB2[top] = PS[2, c2]
    PB1[t10] = PS[1, c1]
    PB0[c0] = PS[0, c0]
    SHARED = 32

    @pl.when(X == 0)
    def _():
        XR[0] = jnp.zeros((8, 2, 16, 128), BF16)
        PH[:, 0:16, :] = jnp.zeros((2, 16, 128), BF16)

    @pl.when(X == 3)
    def _():
        XR[1] = jnp.zeros((8, 2, 16, 128), BF16)
        PH[:, 144:160, :] = jnp.zeros((2, 16, 128), BF16)

    for side, edge_at in ((0, 0), (1, 3)):
        @pl.when(Y == edge_at)
        def _():
            PH[side] = jnp.zeros((160, 128), BF16)
            TABH[side] = jnp.zeros((SHARED, 128), F32)
            PB1H[side] = jnp.zeros((4, 4, 128), F32)
            PB0H[side] = jnp.zeros((2, 4, 128), F32)

    copies = []
    count = [0]

    def plan(src, dst, slot, send_if, take_if, **where):
        copies.append((
            send_if, take_if,
            pltpu.make_async_remote_copy(
                src_ref=src, dst_ref=dst, send_sem=ssem.at[count[0]], recv_sem=rsem.at[slot],
                device_id=where, device_id_type=MESH,
            ),
        ))
        count[0] += 1

    plan(XS.at[1], XR.at[0], 0, x_ok[1], x_ok[0], rng=X + 1)
    plan(XS.at[0], XR.at[1], 1, x_ok[0], x_ok[1], rng=X - 1)
    both = jnp.logical_and
    for side in range(2):
        dy = 1 - 2 * side
        send_y, take_y = y_ok[1 - side], y_ok[side]
        edge = PE.at[1 - side]
        plan(edge, PH.at[side, pl.ds(16, 128), :], 2 + side, send_y, take_y, ang=Y + dy)
        plan(edge.at[pl.ds(112, 16), :], PH.at[side, pl.ds(0, 16), :], 4 + side,
             both(send_y, x_ok[1]), both(take_y, x_ok[0]), rng=X + 1, ang=Y + dy)
        plan(edge.at[pl.ds(0, 16), :], PH.at[side, pl.ds(144, 16), :], 6 + side,
             both(send_y, x_ok[0]), both(take_y, x_ok[1]), rng=X - 1, ang=Y + dy)
        plan(TAB.at[1 - side, pl.ds(0, SHARED), :], TABH.at[side], 8 + side, send_y, take_y, ang=Y + dy)
    sends = []
    takes = ([], [], [])

    def plan_send(src, dst, slot, send_if, **where):
        sends.append((send_if, pltpu.make_async_remote_copy(
            src_ref=src, dst_ref=dst, send_sem=ssem.at[count[0]], recv_sem=rsem.at[slot],
            device_id=where, device_id_type=MESH)))
        count[0] += 1

    def plan_take(lvl, dst, slot, take_if):
        takes[lvl].append((take_if, pltpu.make_async_remote_copy(
            src_ref=dst, dst_ref=dst, send_sem=ssem.at[0], recv_sem=rsem.at[slot],
            device_id=dict(aper=(A + 1) % 32), device_id_type=MESH)))

    for e in range(2):
        plan_send(PS.at[0, e], PB0.at[c0], 22 + c0, c0 != e, aper=4 * (2 * (top // 2) + e) + low)
        plan_take(0, PB0.at[e], 22 + e, c0 != e)
        for side in range(2):
            plan_send(PS.at[0, e, 1 - side], PB0H.at[side, c0], 32 + 2 * side + c0, y_ok[1 - side],
                      aper=4 * (2 * (top // 2) + e) + low, ang=Y + 1 - 2 * side)
            plan_take(0, PB0H.at[side, e], 32 + 2 * side + e, y_ok[side])
    for q in range(4):
        plan_send(PS.at[1, q // 2], PB1.at[t10], 18 + t10, t10 != q, aper=4 * (t2 * 4 + q) + low)
        plan_take(1, PB1.at[q], 18 + q, t10 != q)
        for side in range(2):
            plan_send(PS.at[1, q // 2, 1 - side], PB1H.at[side, t10], 24 + 4 * side + t10, y_ok[1 - side],
                      aper=4 * (t2 * 4 + q) + low, ang=Y + 1 - 2 * side)
            plan_take(1, PB1H.at[side, q], 24 + 4 * side + q, y_ok[side])
    for t in range(8):
        plan_send(PS.at[2, t // 4], PB2.at[top], 10 + top, top != t, aper=4 * t + low)
        plan_take(2, PB2.at[t], 10 + t, top != t)

    pl.semaphore_wait(barrier, 31 + 4 * ny + nx + nx * ny)
    for send_if, _, copy in copies:
        pl.when(send_if)(copy.start)
    for send_if, copy in sends:
        pl.when(send_if)(copy.start)

    k_at = row_of((256, 128))
    near = (jnp.where(k_at < 192, k_at, k_at - 256) - lane_of((256, 128))).astype(F32)
    for lvl in range(3):
        r0 = 16 * lvl
        for b in range(2):
            for h in range(2):
                lag = near - TAB[b, r0 + h:r0 + h + 1, :]
                taps = [TAB[b, r0 + 8 + 4 * h + t:r0 + 9 + 4 * h + t, :] for t in range(4)]
                RHS[lvl, b, :, 128 * h:128 * h + 128] = tap_matrix(lag, taps).astype(BF16)
                rows = shift_rows(TAB[b, r0 + 2 + h:r0 + 3 + h, :], TAB[b, r0 + 4 + h:r0 + 5 + h, :])
                for k, row in enumerate(rows):
                    WT[lvl, h, b, k:k + 1, :] = row

    def ramp_of(first, lvl):
        at = X * 128 - ROWS_BELOW_OUT[lvl] + first + row_of((16, 128))
        inside = jnp.logical_and(at >= 0, at < 512)
        return at.astype(F32) * (1.0 / 512) - 0.5, inside

    def swing(i, carry):
        first = pl.multiple_of(i * 16, 16)
        for lvl in range(3):
            ramp, inside = ramp_of(first, lvl)
            for b in range(2):
                cs = cos_sin(ramp * TAB[b, 16 * lvl + 6:16 * lvl + 7, :])
                for k in range(2):
                    EM[lvl, b, k, pl.ds(first, 16), :] = jnp.where(inside, cs[k], 0.0)
        return carry

    lax.fori_loop(0, 9, swing, 0)

    for _, take_if, copy in copies:
        pl.when(take_if)(copy.wait_recv)

    lane1 = lane_of((1, 128))
    k_q = jnp.where(k_at < 64, 256 + k_at, jnp.where(k_at < 192, k_at - 128, k_at))

    def packed(lo, hi, width):
        half = width // 2
        lane = lane_of(lo.shape)
        got = jnp.where(lane < half, pltpu.roll(lo, half, 1), pltpu.roll(hi, half, 1))
        got = jnp.where(lane < width, got, 0.0)
        step = width
        while step < 128:
            got = got + pltpu.roll(got, step, 1)
            step *= 2
        return got

    def beyond_tables(lvl):
        width = 16 >> lvl
        half = width // 2
        r0 = 16 * lvl
        tab = packed(TABH[0, r0:r0 + 16, :], TABH[1, r0:r0 + 16, :], width)

        def pick(first, second):
            return jnp.where(lane1 < 64, tab[first:first + 1], tab[second:second + 1])

        within = lane1 % width
        beam = jnp.where(within < half, within - half, 256 + within - half)
        lag = (k_q - beam).astype(F32) - pick(0, 1)
        full = tap_matrix(lag, [pick(8 + t, 12 + t) for t in range(4)])
        source = (lane1 // width) % (4 << lvl)
        dest = RHSH0 if lvl == 0 else RHSH1
        for m in range(4 << lvl):
            dest[m] = jnp.where(source == m, full, 0.0).astype(BF16)
        for k, row in enumerate(shift_rows(pick(2, 3), pick(4, 5))):
            WTH[lvl, k:k + 1, :] = row
        known = jnp.where(within < half, one(y_ok[0]), one(y_ok[1])) > 0

        def swing_halo(i, carry, lvl=lvl, rate=tab[6:7], known=known):
            first = pl.multiple_of(i * 16, 16)
            ramp, inside = ramp_of(first, lvl)
            cs = cos_sin(ramp * rate)
            ok = jnp.logical_and(inside, known)
            for k in range(2):
                EH[lvl, k, pl.ds(first, 16), :] = jnp.where(ok, cs[k], 0.0)
            return carry

        lax.fori_loop(0, 9, swing_halo, 0)

    def beyond_phases(lvl):
        width = 16 >> lvl
        owner = lane1 // width
        total = jnp.zeros((1, 128), F32)
        for q in range(2 << lvl):
            lo, hi = (PB0H[0, q], PB0H[1, q]) if lvl == 0 else (PB1H[0, q], PB1H[1, q])
            rows = packed(lo, hi, width)
            mine = 4 * q + row_of((4, 128)) == owner
            total = total + jnp.sum(jnp.where(mine, rows, 0.0), axis=0, keepdims=True)
        cs = cos_sin(total)
        for k in range(2):
            PCH[lvl, k, 0:1, :] = cs[k]

    left_half = lane_of((16, 128)) < 64

    def lay(dest, row, main0, main1, halo, beyond, main_too=True):
        rows = pl.ds(row, 16)
        if main_too:
            dest[0, rows, 0:128] = main0
            dest[1, rows, 0:128] = main1
        dest[0, rows, 128:256] = jnp.where(left_half, main1, halo)
        dest[1, rows, 128:256] = jnp.where(left_half, halo, main0)
        if beyond:
            dest[2, rows, 0:128] = halo
            dest[2, rows, 128:256] = jnp.where(left_half, main0, main1)

    for j in range(4):
        for ri in range(2):
            img = 2 * j + ri
            for first in range(0, 160, 16):
                lo = pltpu.roll(PH[0, first:first + 16, :].astype(F32), (128 - 16 * img - 16) % 128, 1)
                hi = pltpu.roll(PH[1, first:first + 16, :].astype(F32), (128 - 16 * img) % 128, 1)
                halo = jnp.where(left_half, hi, lo).astype(BF16)
                row = 320 * j + 160 * ri + first
                edge = first in (0, 144)
                main = [XR[first // 144, img, b] if edge else L0[b, row:row + 16, 0:128] for b in range(2)]
                lay(L0, row, main[0], main[1], halo, True, edge)

    def settle(src, at, dst, to, b4, b2, lvl, rows):
        d = ROWS_BELOW_IN[lvl] - ROWS_BELOW_OUT[lvl]
        for first in range(0, rows, 8):
            a, b, c, e = (src[at + (pl.ds(first + d + o, 8), slice(None))] for o in (-4, -2, 0, 2))
            dst[to + (pl.ds(first, 8), slice(None))] = jnp.where(b2, jnp.where(b4, e, b), jnp.where(b4, c, a))

    def three(src, at, first, w):
        return (
            w[0] * src[at + (pl.ds(first, 16), slice(None))]
            + w[1] * src[at + (pl.ds(first + 1, 16), slice(None))]
            + w[2] * src[at + (pl.ds(first + 2, 16), slice(None))]
        )

    def turn(re, im, c, s):
        return re * c - im * s, re * s + im * c

    for lvl in range(2):
        src, dst, tail = (L0, L1, RHSH0) if lvl == 0 else (L1, L2, RHSH1)
        rows = ROWS_IN[lvl]
        images = 4 << lvl
        width = 16 >> lvl
        phases = PC0 if lvl == 0 else PC1

        beyond_tables(lvl)
        for take_if, copy in takes[lvl]:
            pl.when(take_if)(copy.wait_recv)
        beyond_phases(lvl)
        if lvl == 0:
            for h0 in range(2):
                for b in range(2):
                    cs = cos_sin(PB0[h0, b])
                    PC0[h0, b, 0], PC0[h0, b, 1] = cs
        else:
            for q in range(4):
                for b in range(2):
                    cs = cos_sin(PB1[q, b])
                    PC1[q, b, 0], PC1[q, b, 1] = cs
        got = dot(src[2, 0:2 * rows, :], tail[0])
        for m in range(1, images):
            got = got + dot(src[2, 2 * rows * m:2 * rows * m + 2 * rows, :], tail[m])
        for ri in range(2):
            IH[ri, 0:rows, :] = got[rows * ri:rows * ri + rows]
            settle(IH, (ri,), S2H, (ri,), WTH[lvl, 0:1, :] > 0.5, WTH[lvl, 1:2, :] > 0.5, lvl, 152)
        w = [WTH[lvl, k:k + 1, :] for k in (2, 3, 4)]
        for first in range(0, 144, 16):
            re, im = three(S2H, (0,), first, w), three(S2H, (1,), first, w)
            re, im = turn(re, im, EH[lvl, 0, first:first + 16, :], EH[lvl, 1, first:first + 16, :])
            re, im = turn(re, im, PCH[lvl, 0, 0:1, :], PCH[lvl, 1, 0:1, :])
            HB[0, first:first + 16, :] = re
            HB[1, first:first + 16, :] = im

        def two_images(i, carry, lvl=lvl, src=src, dst=dst, rows=rows, images=images, width=width, phases=phases):
            for u in range(2):
                at = (2 * i + u) * (2 * rows)
                for b in range(2):
                    got = dot(src[b, pl.ds(at, 2 * rows), :], RHS[lvl, b])
                    for h in range(2):
                        for ri in range(2):
                            IB[u, b, h, ri, 0:rows, :] = got[rows * ri:rows * ri + rows, 128 * h:128 * h + 128]
            for u in range(2):
                m = 2 * i + u
                q = m // 4
                j = m % 4
                w, turned, back = [], [], []
                for h in range(2):
                    for b in range(2):
                        b4 = WT[lvl, h, b, 0:1, :] > 0.5
                        b2 = WT[lvl, h, b, 1:2, :] > 0.5
                        for ri in range(2):
                            settle(IB, (u, b, h, ri), S2, (u, h, b, ri), b4, b2, lvl, 152)
                    w.append([[WT[lvl, h, b, k:k + 1, :] for k in (2, 3, 4)] for b in range(2)])
                    who = h if lvl == 0 else 2 * h + q
                    turned.append([[phases[who, b, k, pl.ds(j, 1), :] for k in range(2)] for b in range(2)])
                    back.append(128 - (width * (images * h + m) + width // 2))
                for first in range(0, 144, 16):
                    swings = [[EM[lvl, b, k, first:first + 16, :] for k in range(2)] for b in range(2)]
                    for h in range(2):
                        main = []
                        for b in range(2):
                            re, im = three(S2, (u, h, b, 0), first, w[h][b]), three(S2, (u, h, b, 1), first, w[h][b])
                            re, im = turn(re, im, swings[b][0], swings[b][1])
                            main.append(turn(re, im, turned[h][b][0], turned[h][b][1]))
                        for ri in range(2):
                            halo = pltpu.roll(HB[ri, first:first + 16, :], back[h], 1).astype(BF16)
                            row = (images * h + m) * 288 + 144 * ri + first
                            lay(dst, row, main[0][ri].astype(BF16), main[1][ri].astype(BF16), halo, lvl == 0)
            return carry

        for i in range(images // 2):
            two_images(i, 0)

    for take_if, copy in takes[2]:
        pl.when(take_if)(copy.wait_recv)
    for t in range(8):
        group = fp[16 * t:16 * t + 16, :]
        mine = group[0:4]
        for k in range(1, 4):
            mine = jnp.where(low == k, group[4 * k:4 * k + 4], mine)
        for b in range(2):
            cs = cos_sin(PB2[t, b] + mine[:, 128 * b:128 * b + 128])
            PC2[t, b, 0], PC2[t, b, 1] = cs

    def rs_copy(k):
        return pltpu.make_async_remote_copy(
            src_ref=SB.at[k], dst_ref=RS.at[A], send_sem=rs_ssem, recv_sem=rs_rsem,
            device_id=dict(aper=k), device_id_type=MESH)

    own_half = A // 16
    for step in range(2):
        b = step
        for i in range(4):
            got = dot(L2[b, 1152 * i:1152 * i + 1152, :], RHS[2, b])
            for h in range(2):
                c = [PC2[4 * h + i, b, 0, j:j + 1, :] for j in range(4)]
                s = [PC2[4 * h + i, b, 1, j:j + 1, :] for j in range(4)]
                for first in range(0, 136, 8):
                    if i:
                        re, im = ACC[h, 0, first:first + 8, :], ACC[h, 1, first:first + 8, :]
                    for j in range(4):
                        row = 288 * j + first
                        x = got[row:row + 8, 128 * h:128 * h + 128]
                        y = got[row + 144:row + 152, 128 * h:128 * h + 128]
                        x, y = turn(x, y, c[j], s[j])
                        re, im = (re + x, im + y) if i or j else (x, y)
                    ACC[h, 0, first:first + 8, :] = re
                    ACC[h, 1, first:first + 8, :] = im
        for h in range(2):
            b4 = WT[2, h, b, 0:1, :] > 0.5
            b2 = WT[2, h, b, 1:2, :] > 0.5
            for ri in range(2):
                settle(ACC, (h, ri), S2, (step, h, 0, ri), b4, b2, 2, 136)
        w = [[WT[2, h, b, k:k + 1, :] for k in (2, 3, 4)] for h in range(2)]
        for first in range(0, 128, 16):
            re = three(S2, (step, 0, 0, 0), first, w[0]) + three(S2, (step, 1, 0, 0), first, w[1])
            im = three(S2, (step, 0, 0, 1), first, w[0]) + three(S2, (step, 1, 0, 1), first, w[1])
            re, im = turn(re, im, EM[2, b, 0, first:first + 16, :], EM[2, b, 1, first:first + 16, :])
            FB[0, first:first + 16, :] = re.astype(BF16)
            FB[1, first:first + 16, :] = im.astype(BF16)
        parts = [lax.dot_general(eye, FB[ri], NT, preferred_element_type=F32).reshape(16, 8, 128) for ri in range(2)]
        SB[pl.ds(16 * b, 16)] = jnp.concatenate(parts, axis=1).astype(BF16)

        def send(i, carry, b=b):
            k = 16 * b + i

            @pl.when(k != A)
            def _():
                rs_copy(k).start()
            return carry

        lax.fori_loop(0, 16, send, 0)

    RS[A] = SB[A]

    for send_if, _, copy in copies:
        pl.when(send_if)(copy.wait_send)
    for send_if, copy in sends:
        pl.when(send_if)(copy.wait_send)

    some = pl.ds(0, 31)
    everything = pltpu.make_async_remote_copy(
        src_ref=SB.at[some], dst_ref=RS.at[some], send_sem=rs_ssem, recv_sem=rs_rsem,
        device_id=dict(aper=(A + 1) % 32), device_id_type=MESH)
    everything.wait_recv()
    parts = [RS[k].astype(F32) for k in range(32)]
    while len(parts) > 1:
        parts = [parts[k] + parts[k + 1] for k in range(0, len(parts), 2)]
    total = parts[0] * (1.0 / math.sqrt(128.0))
    out[0, 0] = total[0:8]
    out[1, 0] = total[8:16]
    everything.wait_send()


def body(*args):
    v = pltpu.VMEM
    return pl.pallas_call(
        kernel,
        out_shape=jax.ShapeDtypeStruct((2, 1, 8, 128), F32),
        in_specs=[pl.BlockSpec(memory_space=pltpu.HBM)] * 8,
        out_specs=pl.BlockSpec(memory_space=pltpu.VMEM),
        scratch_shapes=[v(a.shape, a.dtype) for a in args]
        + [
            pltpu.SemaphoreType.DMA((8,)),
            v((2, 8, 2, 16, 128), BF16),
            v((2, 8, 2, 16, 128), BF16),
            v((2, 128, 128), BF16),
            v((2, 160, 128), BF16),
            v((2, 48, 128), F32),
            v((2, 32, 128), F32),
            v((3, 2, 2, 4, 128), F32),
            v((8, 2, 4, 128), F32),
            v((4, 2, 4, 128), F32),
            v((2, 2, 4, 128), F32),
            v((2, 4, 4, 128), F32),
            v((2, 2, 4, 128), F32),
            v((3, 2, 256, 256), BF16),
            v((4, 256, 128), BF16),
            v((8, 256, 128), BF16),
            v((3, 2, 2, 8, 128), F32),
            v((2, 8, 128), F32),
            v((3, 2, 2, 144, 128), F32),
            v((2, 2, 144, 128), F32),
            v((8, 2, 2, 4, 128), F32),
            v((4, 2, 2, 4, 128), F32),
            v((2, 2, 2, 4, 128), F32),
            v((2, 2, 8, 128), F32),
            v((3, 4 * 320, 256), BF16),
            v((3, 8 * 288, 256), BF16),
            v((2, 16 * 288, 256), BF16),
            v((2, 2, 2, 2, 176, 128), F32),
            v((2, 176, 128), F32),
            v((2, 2, 2, 2, 160, 128), F32),
            v((2, 160, 128), F32),
            v((2, 144, 128), F32),
            v((2, 2, 144, 128), F32),
            v((2, 128, 128), BF16),
            v((32, 16, 128), BF16),
            v((32, 16, 128), BF16),
            pltpu.SemaphoreType.DMA((48,)),
            pltpu.SemaphoreType.DMA((48,)),
            pltpu.SemaphoreType.DMA,
            pltpu.SemaphoreType.DMA,
        ],
        compiler_params=pltpu.CompilerParams(collective_id=0, has_side_effects=True, vmem_limit_bytes=63 * 1024 * 1024),
    )(*args)


def solution(mesh):
    in_specs = (
        P("aper", None, "ang", "rng"),
        P(None, None, None, "ang"),
        P(None, None, None, "ang"),
        P(None, None, None, None, "ang"),
        P(None, None, None, "ang"),
        P("aper", None, None, "ang"),
        P(None, None, "ang"),
        P(None, "ang"),
    )
    out_specs = P(None, "ang", "aper", "rng")
    return jax.shard_map(body, mesh=mesh, in_specs=in_specs, out_specs=out_specs, check_vma=False)
```
